32 devices in a mesh: gx: 4 (over y, core), gy: 2 (over x), gz: 4 (over z).
Axes of the slice: x: 2, y: 2, z: 4, core: 2. Of those that a mesh axis runs over, the one named last changes fastest.
Arguments:
- orbitals: float32 [8, 32, 16, 512], P(None, 'gx', 'gy', 'gz'), may hold values from -6 to 6
- potential: float32 [32, 16, 512], P('gx', 'gy', 'gz'), may hold values from -3 to 0
- proj_values: float32 [4, 65536], P(None, ('gx', 'gy', 'gz')), may hold values from -1 to 1
- point_cell: int32 [65536], P(('gx', 'gy', 'gz')), may hold values from 0 to 8191
- point_owner: int32 [65536], P(('gx', 'gy', 'gz')), may hold values from 0 to 31, as said below
- point_slot: int32 [65536], P(('gx', 'gy', 'gz')), may hold values from 0 to 4
- point_count: int32 [32], P(('gx', 'gy', 'gz')), may hold values from 1 to 2048, 40960 in all
- atom_energy: float32 [4, 160], replicated, may hold values from -2 to 2
Outputs:
- filtered: float32 [8, 32, 16, 512], P(None, 'gx', 'gy', 'gz')
The draws below stay inside these ranges and needn't reach their ends.
Inputs may be any that keep to these rules, and one draw needn't show every extreme that they name: `point_owner`: the owner of point i's atom differs from domain i // 2048 by at most one index along each of gx, gy and gz, counted periodically. Only the first point_count[d] of domain d's 2048 point slots are live; some domain has all of them live.
All inputs are finite; a program needn't handle non-finite values. No bound on the sum of `point_count` on one device may be relied on, other than what follows from the above.
Results may differ from the reference program's by a relative error of at most 0.0001.
Values sent between devices are 32-bit elements; how exact they have to be, the bound alone decides.
A program may use at most 64 MiB of HBM per device.

```python
import math
import jax
import jax.numpy as jnp
import numpy as np
from jax import lax

NORB = 8
NPROJ = 4
DEGREE = 3
CX = 8
CY = 8
CZ = 128
PTS_DEV = 2048
ATOM_DEV = 5
NX = 32
NY = 16
NZ = 512
ATOMS = 160
POINTS = 65536
N_GX = 4
N_GY = 2
N_GZ = 4
DEVICES = 32


def draw_point_owner(key, part):
    key = jax.random.fold_in(key, 7)
    point_total = DEVICES * PTS_DEV
    domain = jnp.arange(point_total, dtype=jnp.int32) // PTS_DEV
    domain_x = domain // (N_GY * N_GZ)
    domain_y = domain // N_GZ % N_GY
    domain_z = domain % N_GZ
    choices_drawn = jax.random.randint(key, (3, point_total), 0, 4)
    moves = jnp.where(choices_drawn < 2, 0, 2 * choices_drawn - 5).astype(jnp.int32)
    owner_x = (domain_x + moves[0]) % N_GX
    owner_y = (domain_y + moves[1]) % N_GY
    owner_z = (domain_z + moves[2]) % N_GZ
    return ((owner_x * N_GY + owner_y) * N_GZ + owner_z).astype(jnp.int32)


def plant(result, own_key, low, top_value):
    longest = result.shape.index(max(result.shape))
    spots = []
    for shift in (0, 1):
        where = [jax.random.randint(jax.random.fold_in(own_key, axis), (), 0, length) for axis, length in enumerate(result.shape)]
        where[longest] = (where[longest] + shift) % result.shape[longest]
        spots.append(tuple(where))
    return result.at[spots[0]].set(low).at[spots[1]].set(top_value)


def levels(key, dims, shards, least, top_value):
    loudness, own = 1.0, jax.random.fold_in(key, 6)
    for position, shards_of in shards:
        heights = jnp.exp(jax.random.uniform(jax.random.fold_in(own, position), (shards_of,), jnp.float32, least / len(shards), top_value / len(shards)))
        loudness = loudness * jnp.repeat(heights, dims[position] // shards_of).reshape([-1 if axis == position else 1 for axis in range(len(dims))])
    return loudness


def split_up(number_of, total, most, lean):
    weights = [(1 << 20) // math.isqrt(grade ** lean) + 1 for grade in range(2, number_of + 1)]
    spare, given = total - most - (number_of - 1), [1] * (number_of - 1)
    while spare > 0:
        free = [i for i in range(number_of - 1) if given[i] < most]
        whole, remaining = sum([weights[i] for i in free]), spare
        for i in free:
            more = min(most - given[i], max(1, remaining * weights[i] // whole), spare)
            given[i] = given[i] + more
            spare = spare - more
    return np.array([most] + given)


def uneven(key, number_of, total, most, skew):
    if number_of == 2:
        one = jax.random.randint(key, (), max(1, total - most), min(most, total - 1) + 1)
        return jnp.stack([one, total - one])
    lengths = jnp.asarray(split_up(number_of, total, most, skew), jnp.int32)
    couples = (number_of - 1) // 2
    giver, sink = lengths[1:1 + 2 * couples:2], lengths[2:2 + 2 * couples:2]
    slack = jnp.minimum(giver - 1, most - sink)
    moved = jax.random.randint(jax.random.fold_in(key, 1), (couples,), 0, 1 << 20) % (slack + 1)
    lengths = lengths.at[1:1 + 2 * couples:2].set(giver - moved).at[2:2 + 2 * couples:2].set(sink + moved)
    return lengths[jax.random.permutation(jax.random.fold_in(key, 2), number_of)]


def scatter_about(key, extent, width, limit, split=(), kind=jnp.bfloat16):
    entries = jax.random.normal(key, extent, jnp.float32) * width
    if len(split) > 0:
        entries = levels(key, extent, split, -0.22, 0.18) * entries
    return jnp.clip(entries, min=-limit, max=limit).astype(kind)


def setup_inputs(seed: int = 0) -> dict:
    key_list = jax.random.split(jax.random.key(seed), 9)
    orbitals = scatter_about(key_list[0], (NORB, NX, NY, NZ), 1.0, 6.0, ((1, 4), (2, 2), (3, 4)), jnp.float32)
    potential = jnp.clip(-3.0 + 3.0 * jax.random.uniform(key_list[1], (NX, NY, NZ), jnp.float32) ** levels(key_list[1], (NX, NY, NZ), ((0, 4), (1, 2), (2, 4)), -0.2, 0.2), -3.0, 0.0)
    proj_values = scatter_about(key_list[2], (NPROJ, POINTS), 0.16, 1.0, ((1, 32),), jnp.float32)
    point_cell = plant(jax.random.randint(key_list[3], (POINTS,), 0, CX * CY * CZ), jax.random.fold_in(key_list[3], 1), 0, (CX * CY * CZ) - 1).astype(jnp.int32)
    point_owner = draw_point_owner(jax.random.fold_in(key_list[8], 71), 0)
    point_slot = plant(jax.random.randint(key_list[5], (POINTS,), 0, ATOM_DEV), jax.random.fold_in(key_list[5], 1), 0, ATOM_DEV - 1).astype(jnp.int32)
    point_count = uneven(key_list[6], DEVICES, DEVICES * PTS_DEV * 5 // 8, PTS_DEV, 2).astype(jnp.int32)
    atom_energy = jnp.clip(jax.random.uniform(key_list[7], (NPROJ, ATOMS), jnp.float32, -2.0, 2.0), -2.0, 2.0)
    return {"orbitals": orbitals, "potential": potential, "proj_values": proj_values, "point_cell": point_cell, "point_owner": point_owner, "point_slot": point_slot, "point_count": point_count, "atom_energy": atom_energy}


stencil_terms = (-5369.0 / 1800.0, 12.0 / 7.0, -15.0 / 56.0, 10.0 / 189.0, -1.0 / 112.0, 2.0 / 1925.0, -1.0 / 16632.0)
lowest = -3.5
cutoff = 1.5
highest = 13.0


def second_sum(padded, along_dim, length):
    def window(first_index):
        return lax.slice_in_dim(padded, first_index, first_index + length, axis=along_dim)

    summed = stencil_terms[0] * window(6)
    for offset in range(1, 7):
        summed = summed + stencil_terms[offset] * (window(6 + offset) + window(6 - offset))
    return summed


def reference(orbitals, potential, proj_values, point_cell, point_owner, point_slot, point_count, atom_energy):
    point_ids = jnp.arange(POINTS, dtype=jnp.int32)
    domain = point_ids // PTS_DEV
    domain_x = domain // (N_GY * N_GZ)
    domain_y = (domain // N_GZ) % N_GY
    domain_z = domain % N_GZ
    local_x = point_cell // (CY * CZ)
    local_y = (point_cell // CZ) % CY
    local_z = point_cell % CZ
    global_cell = ((domain_x * CX + local_x) * NY + domain_y * CY + local_y) * NZ + domain_z * CZ + local_z
    live_mask = ((point_ids % PTS_DEV) < point_count[domain]).astype(jnp.float32)
    masked = proj_values * live_mask[None, :]
    atom_index = point_owner * ATOM_DEV + point_slot

    def hamiltonian(grid_field):
        laplace = second_sum(jnp.pad(grid_field, ((6, 6), (0, 0), (0, 0)), mode="wrap"), 0, NX)
        laplace = laplace + second_sum(jnp.pad(grid_field, ((0, 0), (6, 6), (0, 0)), mode="wrap"), 1, NY)
        laplace = laplace + second_sum(jnp.pad(grid_field, ((0, 0), (0, 0), (6, 6)), mode="wrap"), 2, NZ)
        flattened = grid_field.reshape(-1)
        sampled = flattened[global_cell]
        contributions = (masked * sampled[None, :]).T
        alphas = jax.ops.segment_sum(contributions, atom_index, num_segments=ATOMS)
        coefficients = alphas * atom_energy.T
        returned = jnp.sum(masked.T * coefficients[atom_index], axis=1)
        nonlocal_term = jnp.zeros_like(flattened).at[global_cell].add(returned).reshape(grid_field.shape)
        return -0.5 * laplace + potential * grid_field + nonlocal_term

    def filter_one(grid_field):
        half_width = (highest - cutoff) / 2.0
        middle = (highest + cutoff) / 2.0
        sigma_first = half_width / (lowest - middle)
        previous = grid_field
        current = (sigma_first / half_width) * (hamiltonian(grid_field) - middle * grid_field)
        sigma_now = sigma_first
        for degree_index in range(1, DEGREE):
            sigma_next = 1.0 / (2.0 / sigma_first - sigma_now)
            following = (2.0 * sigma_next / half_width) * (hamiltonian(current) - middle * current) - (sigma_now * sigma_next) * previous
            previous = current
            current = following
            sigma_now = sigma_next
        return current

    return lax.map(filter_one, orbitals)
```

```python
import functools

import jax
import jax.numpy as jnp
from jax import lax
from jax.experimental import pallas as pl
from jax.experimental.pallas import tpu as pltpu
from jax.sharding import PartitionSpec as P

DEGREE = 3
ATOM_DEV = 5
WIDTH = 6
CHUNK = 512
MESH = pl.DeviceIdType.MESH
F32 = jnp.float32
BF16 = jnp.bfloat16
EXACT = lax.Precision.HIGHEST

stencil_terms = (
    -5369.0 / 1800.0,
    12.0 / 7.0,
    -15.0 / 56.0,
    10.0 / 189.0,
    -1.0 / 112.0,
    2.0 / 1925.0,
    -1.0 / 16632.0,
)
lowest = -3.5
cutoff = 1.5
highest = 13.0


def step_factors():
    half = (highest - cutoff) / 2.0
    middle = (highest + cutoff) / 2.0
    first = half / (lowest - middle)
    factors = [(first / half, 0.0)]
    sigma = first
    for _ in range(1, DEGREE):
        following = 1.0 / (2.0 / first - sigma)
        factors.append((2.0 * following / half, -sigma * following))
        sigma = following
    return middle, factors


def split_two(value):
    high = value.astype(BF16)
    low = (value - high.astype(F32)).astype(BF16)
    return high, low


def by_distance(distance):
    result = jnp.zeros(distance.shape, F32)
    for offset in range(WIDTH + 1):
        weight = 0.0 if offset == 0 else -0.5 * stencil_terms[offset]
        result = jnp.where(jnp.abs(distance) == offset, weight, result)
    return result


def kernel(
    sizes,
    orb_ref, pot_ref, val_ref, cell_ref, owner_ref, slot_ref, count_ref, energy_ref,
    out_ref,
    field, x_low, x_high, y_in, z_out, z_in, part_out, part_in, coef_out, coef_in,
    lane_hot, row_hot, seg_hot, masked, send_sem, recv_sem,
):
    size_x, size_y, size_z = sizes
    norb, cx, cy, cz = orb_ref.shape
    nproj, points = val_ref.shape
    rows = cx * cy
    spans = [min(3, size) for size in sizes]
    codes = [(a, b, c) for a in range(spans[0]) for b in range(spans[1]) for c in range(spans[2])]
    blocks = len(codes)
    seg_rows = seg_hot.shape[0]
    here = [lax.axis_index(name) for name in ("gx", "gy", "gz")]
    names = ("gx", "gy", "gz")

    def moved(axis, code):
        step = (0, 1, sizes[axis] - 1)[code]
        return lax.rem(here[axis] + step, sizes[axis])

    def device(code):
        return {name: moved(axis, code[axis]) for axis, name in enumerate(names)}

    def opposite(code):
        back = [0 if c == 0 else (1 if sizes[a] == 2 else 3 - c) for a, c in enumerate(code)]
        return codes.index(tuple(back))

    barrier = pltpu.get_barrier_semaphore()
    for code in codes[1:]:
        pl.semaphore_signal(barrier, inc=1, device_id=device(code), device_id_type=MESH)

    cells = cell_ref[...]
    lanes_of = cells % cz
    rows_of = cells // cz
    at_lane = (lax.broadcasted_iota(jnp.int32, (cz, points), 0) == lanes_of).astype(F32).astype(BF16)
    lane_hot[0:cz, :] = at_lane
    lane_hot[cz:2 * cz, :] = at_lane
    row_hot[...] = (lax.broadcasted_iota(jnp.int32, (rows, points), 0) == rows_of).astype(F32)
    owner = owner_ref[...]
    coords = (owner // (size_y * size_z), owner // size_z % size_y, owner % size_z)
    block = jnp.zeros_like(owner)
    for axis in range(3):
        remain = (coords[axis] - here[axis] + sizes[axis]) % sizes[axis]
        block = block * spans[axis] + jnp.minimum(remain, 2)
    segment = block * 8 + slot_ref[...]
    seg_hot[...] = (
        lax.broadcasted_iota(jnp.int32, (seg_rows, points), 0) == segment
    ).astype(F32).astype(BF16)
    live = lax.broadcasted_iota(jnp.int32, (nproj, points), 1) < count_ref[0]
    masked[...] = jnp.where(live, val_ref[...], 0.0)

    atoms = energy_ref.shape[1]
    domain = (here[0] * size_y + here[1]) * size_z + here[2]
    slots = lax.broadcasted_iota(jnp.int32, (8, atoms), 0)
    mine = (lax.broadcasted_iota(jnp.int32, (8, atoms), 1) == domain * ATOM_DEV + slots) & (
        slots < ATOM_DEV
    )
    lane_group = lax.broadcasted_iota(jnp.int32, (8, 128), 1) // norb
    energies = jnp.zeros((8, 128), F32)
    for j in range(nproj):
        own = jnp.sum(jnp.where(mine, energy_ref[j:j + 1, :], 0.0), axis=1, keepdims=True)
        energies = jnp.where(lane_group == j, own, energies)

    first = lax.broadcasted_iota(jnp.int32, (cz, cz), 0)
    second = lax.broadcasted_iota(jnp.int32, (cz, cz), 1)
    band = by_distance(first - second)
    place = lax.broadcasted_iota(jnp.int32, (16, cz), 0)
    lane = lax.broadcasted_iota(jnp.int32, (16, cz), 1)
    edge_band = by_distance(jnp.where(place < 8, place - 8, place - 8 + cz) - lane)
    edge_pick = (lane == jnp.where(place < 8, place, place - 16 + cz)).astype(F32)

    pl.semaphore_wait(barrier, blocks - 1)

    middle, factors = step_factors()
    started = []

    def send(step, index, source, target, device_id):
        copy = pltpu.make_async_remote_copy(
            src_ref=source,
            dst_ref=target,
            send_sem=send_sem.at[step, index],
            recv_sem=recv_sem.at[step, index],
            device_id=device_id,
            device_id_type=MESH,
        )
        copy.start()
        started.append(copy)
        return copy

    for step in range(DEGREE):
        source = orb_ref if step == 0 else field.at[step - 1]
        up = [{names[axis]: moved(axis, 1)} for axis in range(3)]
        down = [{names[axis]: lax.rem(here[axis] + sizes[axis] - 1, sizes[axis])} for axis in range(3)]
        y_copies = [send(step, 2, source, y_in.at[step, 0], up[1])]
        if size_y > 2:
            y_copies.append(send(step, 3, source, y_in.at[step, 1], down[1]))
        x_copies = [
            send(step, 0, source.at[:, pl.ds(cx - WIDTH, WIDTH)], x_low.at[step], up[0]),
            send(step, 1, source.at[:, pl.ds(0, WIDTH)], x_high.at[step], down[0]),
        ]
        flat = source[...].reshape(norb * rows, cz)
        z_out[step] = lax.dot_general(
            edge_pick, flat, (((1,), (1,)), ((), ())), precision=EXACT, preferred_element_type=F32
        ).reshape(2, 8, norb * rows)
        z_copies = [
            send(step, 4, z_out.at[step, 1], z_in.at[step, 0], up[2]),
            send(step, 5, z_out.at[step, 0], z_in.at[step, 1], down[2]),
        ]

        high, low = split_two(flat)
        both = jnp.concatenate([high, low], axis=1)
        weighted = []
        for begin in range(0, points, CHUNK):
            span = slice(begin, begin + CHUNK)
            spread = jnp.dot(both, lane_hot[:, span], preferred_element_type=F32)
            sampled = jnp.sum(
                spread.reshape(norb, rows, CHUNK) * row_hot[:, span][None], axis=1
            )
            weighted.append(
                jnp.concatenate([sampled * masked[j:j + 1, span] for j in range(nproj)], axis=0)
            )
        weighted = jnp.concatenate(weighted, axis=1)
        high, low = split_two(weighted)
        filler = jnp.zeros((128 - 2 * nproj * norb, points), BF16)
        partial = lax.dot_general(
            seg_hot[...],
            jnp.concatenate([high, low, filler], axis=0),
            (((1,), (1,)), ((), ())),
            preferred_element_type=F32,
        )
        partial = partial + pltpu.roll(partial, 128 - nproj * norb, 1)
        part_out[step] = partial[0:blocks * 8].reshape(blocks, 8, 128)
        part_copies = [
            send(step, 6 + n, part_out.at[step, n], part_in.at[step, n], device(codes[n]))
            for n in range(1, blocks)
        ]

        local = (pot_ref[...][None] + (-1.5 * stencil_terms[0] - middle)) * source[...]
        local = local + jnp.dot(
            flat, band, precision=EXACT, preferred_element_type=F32
        ).reshape(norb, cx, cy, cz)
        for copy in z_copies:
            copy.wait_recv()
        edges = z_in[step].reshape(16, norb * rows)
        local = local + jnp.dot(
            edges.T, edge_band, precision=EXACT, preferred_element_type=F32
        ).reshape(norb, cx, cy, cz)

        owned = partial[0:8]
        for n, copy in enumerate(part_copies, 1):
            copy.wait_recv()
            owned = owned + part_in[step, n]
        coefficients = owned * energies
        coef_out[step] = coefficients
        coef_copies = [
            send(
                step, 6 + blocks + n, coef_out.at[step], coef_in.at[step, opposite(codes[n])],
                device(codes[n]),
            )
            for n in range(1, blocks)
        ]

        for copy in x_copies:
            copy.wait_recv()
        along = jnp.concatenate([x_low[step], source[...], x_high[step]], axis=1)
        for offset in range(1, WIDTH + 1):
            local = local + (-0.5 * stencil_terms[offset]) * (
                along[:, WIDTH + offset:WIDTH + offset + cx]
                + along[:, WIDTH - offset:WIDTH - offset + cx]
            )
        for copy in y_copies:
            copy.wait_recv()
        below = y_in[step, 0]
        above = below if size_y == 2 else y_in[step, 1]
        along = jnp.concatenate([below, source[...], above], axis=2)
        for offset in range(1, WIDTH + 1):
            local = local + (-0.5 * stencil_terms[offset]) * (
                along[:, :, cy + offset:2 * cy + offset] + along[:, :, cy - offset:2 * cy - offset]
            )

        for copy in coef_copies:
            copy.wait_recv()
        around = jnp.concatenate(
            [coefficients]
            + [coef_in[step, n] for n in range(1, blocks)]
            + [jnp.zeros((seg_rows - 8 * blocks, 128), F32)],
            axis=0,
        )
        high, low = split_two(around.T[0:nproj * norb])
        spread = jnp.dot(
            jnp.concatenate([high, low], axis=0), seg_hot[...], preferred_element_type=F32
        )
        spread = spread[0:nproj * norb] + spread[nproj * norb:2 * nproj * norb]
        returned = spread[0:norb] * masked[0:1, :]
        for j in range(1, nproj):
            returned = returned + spread[j * norb:(j + 1) * norb] * masked[j:j + 1, :]
        high, low = split_two(returned)
        high, low = high.astype(F32), low.astype(F32)
        scattered = jnp.zeros((norb * rows, cz), F32)
        for begin in range(0, points, CHUNK):
            span = slice(begin, begin + CHUNK)
            for term in (high, low):
                spots = (term[:, None, span] * row_hot[:, span][None]).astype(BF16)
                scattered = scattered + lax.dot_general(
                    spots.reshape(norb * rows, CHUNK),
                    lane_hot[0:cz, span],
                    (((1,), (1,)), ((), ())),
                    preferred_element_type=F32,
                )
        scale, keep = factors[step]
        result = scale * (local + scattered.reshape(norb, cx, cy, cz))
        if step > 0:
            previous = orb_ref if step == 1 else field.at[step - 2]
            result = result + keep * previous[...]
        if step < DEGREE - 1:
            field[step] = result
        else:
            out_ref[...] = result

    for copy in started:
        copy.wait_send()


def body(sizes, orbitals, potential, proj_values, point_cell, point_owner, point_slot, point_count, atom_energy):
    norb, cx, cy, cz = orbitals.shape
    nproj, points = proj_values.shape
    rows = cx * cy
    blocks = 1
    for size in sizes:
        blocks = blocks * min(3, size)
    seg_rows = (8 * blocks + 127) // 128 * 128
    copies = 6 + 2 * blocks
    vmem = pl.BlockSpec(memory_space=pltpu.VMEM)
    smem = pl.BlockSpec(memory_space=pltpu.SMEM)
    return pl.pallas_call(
        functools.partial(kernel, sizes),
        out_shape=jax.ShapeDtypeStruct(orbitals.shape, F32),
        in_specs=[vmem] * 6 + [smem, vmem],
        out_specs=vmem,
        scratch_shapes=[
            pltpu.VMEM((DEGREE - 1, norb, cx, cy, cz), F32),
            pltpu.VMEM((DEGREE, norb, WIDTH, cy, cz), F32),
            pltpu.VMEM((DEGREE, norb, WIDTH, cy, cz), F32),
            pltpu.VMEM((DEGREE, 1 if sizes[1] == 2 else 2, norb, cx, cy, cz), F32),
            pltpu.VMEM((DEGREE, 2, 8, norb * rows), F32),
            pltpu.VMEM((DEGREE, 2, 8, norb * rows), F32),
            pltpu.VMEM((DEGREE, blocks, 8, 128), F32),
            pltpu.VMEM((DEGREE, blocks, 8, 128), F32),
            pltpu.VMEM((DEGREE, 8, 128), F32),
            pltpu.VMEM((DEGREE, blocks, 8, 128), F32),
            pltpu.VMEM((2 * cz, points), BF16),
            pltpu.VMEM((rows, points), F32),
            pltpu.VMEM((seg_rows, points), BF16),
            pltpu.VMEM((nproj, points), F32),
            pltpu.SemaphoreType.DMA((DEGREE, copies)),
            pltpu.SemaphoreType.DMA((DEGREE, copies)),
        ],
        compiler_params=pltpu.CompilerParams(
            collective_id=0, has_side_effects=True, vmem_limit_bytes=48 * 1024 * 1024
        ),
    )(
        orbitals,
        potential,
        proj_values,
        point_cell.reshape(1, points),
        point_owner.reshape(1, points),
        point_slot.reshape(1, points),
        point_count,
        atom_energy,
    )


def solution(mesh):
    sizes = tuple(mesh.shape[name] for name in ("gx", "gy", "gz"))
    return jax.shard_map(
        functools.partial(body, sizes),
        mesh=mesh,
        in_specs=(
            P(None, "gx", "gy", "gz"),
            P("gx", "gy", "gz"),
            P(None, ("gx", "gy", "gz")),
            P(("gx", "gy", "gz")),
            P(("gx", "gy", "gz")),
            P(("gx", "gy", "gz")),
            P(("gx", "gy", "gz")),
            P(),
        ),
        out_specs=P(None, "gx", "gy", "gz"),
        check_vma=False,
    )
```

```python
import functools

import jax
import jax.numpy as jnp
from jax import lax
from jax.experimental import pallas as pl
from jax.experimental.pallas import tpu as pltpu
from jax.sharding import PartitionSpec as P

DEGREE = 3
ATOM_DEV = 5
WIDTH = 6
CHUNK = 512
GROUPS = 1
MESH = pl.DeviceIdType.MESH
F32 = jnp.float32
BF16 = jnp.bfloat16

stencil_terms = (
    -5369.0 / 1800.0,
    12.0 / 7.0,
    -15.0 / 56.0,
    10.0 / 189.0,
    -1.0 / 112.0,
    2.0 / 1925.0,
    -1.0 / 16632.0,
)
lowest = -3.5
cutoff = 1.5
highest = 13.0


def step_factors():
    half = (highest - cutoff) / 2.0
    middle = (highest + cutoff) / 2.0
    first = half / (lowest - middle)
    factors = [(first / half, 0.0)]
    sigma = first
    for _ in range(1, DEGREE):
        following = 1.0 / (2.0 / first - sigma)
        factors.append((2.0 * following / half, -sigma * following))
        sigma = following
    return middle, factors


def split_two(value):
    high = value.astype(BF16)
    low = (value - high.astype(F32)).astype(BF16)
    return high, low


def by_distance(distance):
    result = jnp.zeros(distance.shape, F32)
    for offset in range(WIDTH + 1):
        weight = 0.0 if offset == 0 else -0.5 * stencil_terms[offset]
        result = jnp.where(jnp.abs(distance) == offset, weight, result)
    return result


def kernel(
    sizes, groups,
    orb_hbm, pot_hbm, val_hbm, cell_hbm, owner_hbm, slot_hbm, count_ref, energy_hbm,
    out_ref,
    orb_ref, pot_ref, val_ref, cell_ref, owner_ref, slot_ref, energy_ref,
    field, acc, x_low, x_high, y_in, z_out, z_in, part_out, part_in, coef_out, coef_in,
    lane_hot, row_hot, seg_hot, masked, load_sem, send_sem, recv_sem,
):
    size_x, size_y, size_z = sizes
    norb, cx, cy, cz = orb_ref.shape
    nproj, points = val_ref.shape
    rows = cx * cy
    each = norb // groups
    spans = [min(3, size) for size in sizes]
    codes = [(a, b, c) for a in range(spans[0]) for b in range(spans[1]) for c in range(spans[2])]
    blocks = len(codes)
    seg_rows = seg_hot.shape[0]
    here = [lax.axis_index(name) for name in ("gx", "gy", "gz")]
    names = ("gx", "gy", "gz")

    loads = [
        pltpu.make_async_copy(source, target, load_sem.at[n])
        for n, (source, target) in enumerate(
            [
                (orb_hbm, orb_ref),
                (cell_hbm, cell_ref),
                (owner_hbm, owner_ref),
                (slot_hbm, slot_ref),
                (val_hbm, val_ref),
                (energy_hbm, energy_ref),
                (pot_hbm, pot_ref),
            ]
        )
    ]
    for load in loads:
        load.start()

    def moved(axis, code):
        step = (0, 1, sizes[axis] - 1)[code]
        return lax.rem(here[axis] + step, sizes[axis])

    def device(code):
        return {name: moved(axis, code[axis]) for axis, name in enumerate(names)}

    def opposite(code):
        back = [0 if c == 0 else (1 if sizes[a] == 2 else 3 - c) for a, c in enumerate(code)]
        return codes.index(tuple(back))

    up = [{names[axis]: moved(axis, 1)} for axis in range(3)]
    down = [{names[axis]: lax.rem(here[axis] + sizes[axis] - 1, sizes[axis])} for axis in range(3)]

    barrier = pltpu.get_barrier_semaphore()
    for code in codes[1:]:
        pl.semaphore_signal(barrier, inc=1, device_id=device(code), device_id_type=MESH)

    middle, factors = step_factors()
    started = []

    def send(step, group, index, source, target, device_id):
        copy = pltpu.make_async_remote_copy(
            src_ref=source,
            dst_ref=target,
            send_sem=send_sem.at[step, group, index],
            recv_sem=recv_sem.at[step, group, index],
            device_id=device_id,
            device_id_type=MESH,
        )
        copy.start()
        started.append(copy)
        return copy

    def source_of(step):
        return orb_ref if step == 0 else field.at[step - 1]

    state = {}

    def send_faces(step, group):
        span = pl.ds(group * each, each)
        source = source_of(step)
        y_copies = [
            send(step, group, 2, source.at[span], y_in.at[step, 0, span], up[1])
        ]
        if size_y > 2:
            y_copies.append(send(step, group, 3, source.at[span], y_in.at[step, 1, span], down[1]))
        x_copies = [
            send(
                step, group, 0, source.at[span, pl.ds(cx - WIDTH, WIDTH)], x_low.at[step, span], up[0]
            ),
            send(step, group, 1, source.at[span, pl.ds(0, WIDTH)], x_high.at[step, span], down[0]),
        ]
        state[step, group] = {"x": x_copies, "y": y_copies}

    first = lax.broadcasted_iota(jnp.int32, (cz, cz), 0)
    second = lax.broadcasted_iota(jnp.int32, (cz, cz), 1)
    high, low = split_two(by_distance(first - second))
    band = jnp.concatenate(
        [
            jnp.concatenate([high, low], axis=1),
            jnp.concatenate([high, jnp.zeros_like(low)], axis=1),
        ],
        axis=0,
    )
    place = lax.broadcasted_iota(jnp.int32, (16, cz), 0)
    lane = lax.broadcasted_iota(jnp.int32, (16, cz), 1)
    high, low = split_two(by_distance(jnp.where(place < 8, place - 8, place - 8 + cz) - lane))
    edge_band = jnp.concatenate([high, high, low], axis=0)
    edge_pick = (lane == jnp.where(place < 8, place, place - 16 + cz)).astype(F32).astype(BF16)
    edge_pick = jnp.concatenate([edge_pick, edge_pick], axis=1)

    pl.semaphore_wait(barrier, blocks - 1)
    loads[0].wait()
    for group in range(groups):
        send_faces(0, group)

    for load in loads[1:]:
        load.wait()
    cells = cell_ref[...]
    lanes_of = cells % cz
    rows_of = cells // cz
    at_lane = (lax.broadcasted_iota(jnp.int32, (cz, points), 0) == lanes_of).astype(F32).astype(BF16)
    lane_hot[0:cz, :] = at_lane
    lane_hot[cz:2 * cz, :] = at_lane
    row_hot[...] = (lax.broadcasted_iota(jnp.int32, (rows, points), 0) == rows_of).astype(F32)
    owner = owner_ref[...]
    coords = (owner // (size_y * size_z), owner // size_z % size_y, owner % size_z)
    block = jnp.zeros_like(owner)
    for axis in range(3):
        remain = (coords[axis] - here[axis] + sizes[axis]) % sizes[axis]
        block = block * spans[axis] + jnp.minimum(remain, 2)
    segment = block * 8 + slot_ref[...]
    seg_hot[...] = (
        lax.broadcasted_iota(jnp.int32, (seg_rows, points), 0) == segment
    ).astype(F32).astype(BF16)
    live = lax.broadcasted_iota(jnp.int32, (nproj, points), 1) < count_ref[0]
    masked[...] = jnp.where(live, val_ref[...], 0.0)

    atoms = energy_ref.shape[1]
    domain = (here[0] * size_y + here[1]) * size_z + here[2]
    slots = lax.broadcasted_iota(jnp.int32, (8, atoms), 0)
    mine = (lax.broadcasted_iota(jnp.int32, (8, atoms), 1) == domain * ATOM_DEV + slots) & (
        slots < ATOM_DEV
    )
    lane_group = lax.broadcasted_iota(jnp.int32, (8, 128), 1) // each
    energies = jnp.zeros((8, 128), F32)
    for j in range(nproj):
        own = jnp.sum(jnp.where(mine, energy_ref[j:j + 1, :], 0.0), axis=1, keepdims=True)
        energies = jnp.where(lane_group == j, own, energies)

    used = nproj * each

    def begin(step, group):
        now = state[step, group]
        span = slice(group * each, group * each + each)
        flat = source_of(step)[span].reshape(each * rows, cz)
        high, low = split_two(flat)
        both = jnp.concatenate([high, low], axis=1)
        now["both"] = both
        z_out[step, group] = lax.dot_general(
            edge_pick, both, (((1,), (1,)), ((), ())), preferred_element_type=F32
        ).reshape(2, 8, each * rows)
        now["z"] = [
            send(step, group, 4, z_out.at[step, group, 1], z_in.at[step, group, 0], up[2]),
            send(step, group, 5, z_out.at[step, group, 0], z_in.at[step, group, 1], down[2]),
        ]
        weighted = []
        for start in range(0, points, CHUNK):
            part = slice(start, start + CHUNK)
            spread = jnp.dot(both, lane_hot[:, part], preferred_element_type=F32)
            sampled = jnp.sum(spread.reshape(each, rows, CHUNK) * row_hot[:, part][None], axis=1)
            weighted.append(
                jnp.concatenate([sampled * masked[j:j + 1, part] for j in range(nproj)], axis=0)
            )
        high, low = split_two(jnp.concatenate(weighted, axis=1))
        filler = jnp.zeros((128 - 2 * used, points), BF16)
        partial = lax.dot_general(
            seg_hot[...],
            jnp.concatenate([high, low, filler], axis=0),
            (((1,), (1,)), ((), ())),
            preferred_element_type=F32,
        )
        partial = partial + pltpu.roll(partial, 128 - used, 1)
        now["own"] = partial[0:8]
        part_out[step, group] = partial[0:blocks * 8].reshape(blocks, 8, 128)
        now["part"] = [
            send(
                step, group, 6 + n, part_out.at[step, group, n], part_in.at[step, group, n],
                device(codes[n]),
            )
            for n in range(1, blocks)
        ]

    def along_lanes(step, group):
        now = state[step, group]
        span = slice(group * each, group * each + each)
        total = jnp.dot(now["both"], band, preferred_element_type=F32)
        total = total[:, 0:cz] + total[:, cz:2 * cz]
        for copy in now["z"]:
            copy.wait_recv()
        high, low = split_two(z_in[step, group].reshape(16, each * rows))
        edges = jnp.concatenate([high.astype(F32), low.astype(F32), high.astype(F32)], axis=0)
        total = total + jnp.dot(edges.T.astype(BF16), edge_band, preferred_element_type=F32)
        acc[span] = total.reshape(each, cx, cy, cz)

    def give_back(step, group):
        now = state[step, group]
        owned = now["own"]
        for n, copy in enumerate(now["part"], 1):
            copy.wait_recv()
            owned = owned + part_in[step, group, n]
        coefficients = owned * energies
        now["own"] = coefficients
        coef_out[step, group] = coefficients
        now["coef"] = [
            send(
                step, group, 6 + blocks + n, coef_out.at[step, group],
                coef_in.at[step, group, opposite(codes[n])], device(codes[n]),
            )
            for n in range(1, blocks)
        ]

    def across_rows(step, group):
        now = state[step, group]
        for copy in now["x"] + now["y"]:
            copy.wait_recv()
        source = source_of(step)
        for o in range(group * each, group * each + each):
            own = source[o]
            total = acc[o] + (pot_ref[...] + (-1.5 * stencil_terms[0] - middle)) * own
            below = y_in[step, 0, o]
            above = below if size_y == 2 else y_in[step, 1, o]
            in_x = jnp.concatenate([x_low[step, o], own, x_high[step, o]], axis=0)
            in_y = jnp.concatenate([below, own, above], axis=1)
            for k in range(1, WIDTH + 1):
                total = total + (-0.5 * stencil_terms[k]) * (
                    (in_x[WIDTH + k:WIDTH + k + cx] + in_x[WIDTH - k:WIDTH - k + cx])
                    + (in_y[:, cy + k:2 * cy + k] + in_y[:, cy - k:2 * cy - k])
                )
            acc[o] = total

    def finish(step, group):
        now = state[step, group]
        for copy in now["coef"]:
            copy.wait_recv()
        around = jnp.concatenate(
            [now["own"]]
            + [coef_in[step, group, n] for n in range(1, blocks)]
            + [jnp.zeros((seg_rows - 8 * blocks, 128), F32)],
            axis=0,
        )
        high, low = split_two(around.T[0:used])
        spread = jnp.dot(
            jnp.concatenate([high, low], axis=0), seg_hot[...], preferred_element_type=F32
        )
        spread = spread[0:used] + spread[used:2 * used]
        returned = spread[0:each] * masked[0:1, :]
        for j in range(1, nproj):
            returned = returned + spread[j * each:(j + 1) * each] * masked[j:j + 1, :]
        high, low = split_two(returned)
        high, low = high.astype(F32), low.astype(F32)
        scattered = jnp.zeros((each * rows, cz), F32)
        for start in range(0, points, CHUNK):
            part = slice(start, start + CHUNK)
            at_row = row_hot[:, part].astype(BF16).reshape(1, rows // 16, 16, CHUNK)
            for term in (high, low):
                wide = jnp.broadcast_to(term[:, None, part], (each, 16, CHUNK)).astype(BF16)
                spots = wide[:, None] * at_row
                scattered = scattered + lax.dot_general(
                    spots.reshape(each * rows, CHUNK),
                    lane_hot[0:cz, part],
                    (((1,), (1,)), ((), ())),
                    preferred_element_type=F32,
                )
        scattered = scattered.reshape(each, cx, cy, cz)
        scale, keep = factors[step]
        span = slice(group * each, group * each + each)
        result = scale * (acc[span] + scattered)
        if step > 0:
            result = result + keep * source_of(step - 1)[span]
        if step < DEGREE - 1:
            field[step, span] = result
        else:
            out_ref[span] = result

    everyone = range(groups)
    for group in everyone:
        begin(0, group)
    for step in range(DEGREE):
        for group in everyone:
            along_lanes(step, group)
            give_back(step, group)
        for group in everyone:
            across_rows(step, group)
            finish(step, group)
            if step < DEGREE - 1:
                send_faces(step + 1, group)
                begin(step + 1, group)

    for copy in started:
        copy.wait_send()


def body(sizes, orbitals, potential, proj_values, point_cell, point_owner, point_slot, point_count, atom_energy):
    norb, cx, cy, cz = orbitals.shape
    nproj, points = proj_values.shape
    rows = cx * cy
    blocks = 1
    for size in sizes:
        blocks = blocks * min(3, size)
    seg_rows = (8 * blocks + 127) // 128 * 128
    copies = 6 + 2 * blocks
    groups = GROUPS
    each_rows = norb // groups * rows
    vmem = pl.BlockSpec(memory_space=pltpu.VMEM)
    smem = pl.BlockSpec(memory_space=pltpu.SMEM)
    hbm = pl.BlockSpec(memory_space=pltpu.HBM)
    return pl.pallas_call(
        functools.partial(kernel, sizes, groups),
        out_shape=jax.ShapeDtypeStruct(orbitals.shape, F32),
        in_specs=[hbm] * 6 + [smem, hbm],
        out_specs=vmem,
        scratch_shapes=[
            pltpu.VMEM(orbitals.shape, F32),
            pltpu.VMEM(potential.shape, F32),
            pltpu.VMEM(proj_values.shape, F32),
            pltpu.VMEM((1, points), jnp.int32),
            pltpu.VMEM((1, points), jnp.int32),
            pltpu.VMEM((1, points), jnp.int32),
            pltpu.VMEM(atom_energy.shape, F32),
            pltpu.VMEM((DEGREE - 1, norb, cx, cy, cz), F32),
            pltpu.VMEM((norb, cx, cy, cz), F32),
            pltpu.VMEM((DEGREE, norb, WIDTH, cy, cz), F32),
            pltpu.VMEM((DEGREE, norb, WIDTH, cy, cz), F32),
            pltpu.VMEM((DEGREE, 1 if sizes[1] == 2 else 2, norb, cx, cy, cz), F32),
            pltpu.VMEM((DEGREE, groups, 2, 8, each_rows), F32),
            pltpu.VMEM((DEGREE, groups, 2, 8, each_rows), F32),
            pltpu.VMEM((DEGREE, groups, blocks, 8, 128), F32),
            pltpu.VMEM((DEGREE, groups, blocks, 8, 128), F32),
            pltpu.VMEM((DEGREE, groups, 8, 128), F32),
            pltpu.VMEM((DEGREE, groups, blocks, 8, 128), F32),
            pltpu.VMEM((2 * cz, points), BF16),
            pltpu.VMEM((rows, points), F32),
            pltpu.VMEM((seg_rows, points), BF16),
            pltpu.VMEM((nproj, points), F32),
            pltpu.SemaphoreType.DMA((7,)),
            pltpu.SemaphoreType.DMA((DEGREE, groups, copies)),
            pltpu.SemaphoreType.DMA((DEGREE, groups, copies)),
        ],
        compiler_params=pltpu.CompilerParams(
            collective_id=0, has_side_effects=True, vmem_limit_bytes=48 * 1024 * 1024
        ),
    )(
        orbitals,
        potential,
        proj_values,
        point_cell.reshape(1, points),
        point_owner.reshape(1, points),
        point_slot.reshape(1, points),
        point_count,
        atom_energy,
    )


def solution(mesh):
    sizes = tuple(mesh.shape[name] for name in ("gx", "gy", "gz"))
    return jax.shard_map(
        functools.partial(body, sizes),
        mesh=mesh,
        in_specs=(
            P(None, "gx", "gy", "gz"),
            P("gx", "gy", "gz"),
            P(None, ("gx", "gy", "gz")),
            P(("gx", "gy", "gz")),
            P(("gx", "gy", "gz")),
            P(("gx", "gy", "gz")),
            P(("gx", "gy", "gz")),
            P(),
        ),
        out_specs=P(None, "gx", "gy", "gz"),
        check_vma=False,
    )
```

```python
import functools

import jax
import jax.numpy as jnp
from jax import lax
from jax.experimental import pallas as pl
from jax.experimental.pallas import tpu as pltpu
from jax.sharding import PartitionSpec as P

DEGREE = 3
ATOM_DEV = 5
WIDTH = 6
CHUNK = 512
GROUPS = 2
MESH = pl.DeviceIdType.MESH
F32 = jnp.float32
BF16 = jnp.bfloat16

stencil_terms = (
    -5369.0 / 1800.0,
    12.0 / 7.0,
    -15.0 / 56.0,
    10.0 / 189.0,
    -1.0 / 112.0,
    2.0 / 1925.0,
    -1.0 / 16632.0,
)
lowest = -3.5
cutoff = 1.5
highest = 13.0


def step_factors():
    half = (highest - cutoff) / 2.0
    middle = (highest + cutoff) / 2.0
    first = half / (lowest - middle)
    factors = [(first / half, 0.0)]
    sigma = first
    for _ in range(1, DEGREE):
        following = 1.0 / (2.0 / first - sigma)
        factors.append((2.0 * following / half, -sigma * following))
        sigma = following
    return middle, factors


def split_two(value):
    high = value.astype(BF16)
    low = (value - high.astype(F32)).astype(BF16)
    return high, low


def by_distance(distance):
    result = jnp.zeros(distance.shape, F32)
    for offset in range(WIDTH + 1):
        weight = 0.0 if offset == 0 else -0.5 * stencil_terms[offset]
        result = jnp.where(jnp.abs(distance) == offset, weight, result)
    return result


def kernel(
    sizes, groups,
    orb_hbm, pot_hbm, val_hbm, cell_hbm, owner_hbm, slot_hbm, count_ref, energy_hbm,
    out_ref,
    orb_ref, pot_ref, val_ref, cell_ref, owner_ref, slot_ref, energy_ref,
    field, acc, x_low, x_high, y_in, z_out, z_in, part_out, part_in, coef_out, coef_in,
    lane_hot, row_hot, seg_hot, masked, load_sem, send_sem, recv_sem,
):
    size_x, size_y, size_z = sizes
    norb, cx, cy, cz = orb_ref.shape
    nproj, points = val_ref.shape
    rows = cx * cy
    each = norb // groups
    spans = [min(3, size) for size in sizes]
    codes = [(a, b, c) for a in range(spans[0]) for b in range(spans[1]) for c in range(spans[2])]
    blocks = len(codes)
    seg_rows = seg_hot.shape[0]
    here = [lax.axis_index(name) for name in ("gx", "gy", "gz")]
    names = ("gx", "gy", "gz")

    loads = [
        pltpu.make_async_copy(source, target, load_sem.at[n])
        for n, (source, target) in enumerate(
            [
                (orb_hbm, orb_ref),
                (cell_hbm, cell_ref),
                (owner_hbm, owner_ref),
                (slot_hbm, slot_ref),
                (val_hbm, val_ref),
                (energy_hbm, energy_ref),
                (pot_hbm, pot_ref),
            ]
        )
    ]
    for load in loads:
        load.start()

    def moved(axis, code):
        step = (0, 1, sizes[axis] - 1)[code]
        return lax.rem(here[axis] + step, sizes[axis])

    def device(code):
        return {name: moved(axis, code[axis]) for axis, name in enumerate(names)}

    def opposite(code):
        back = [0 if c == 0 else (1 if sizes[a] == 2 else 3 - c) for a, c in enumerate(code)]
        return codes.index(tuple(back))

    up = [{names[axis]: moved(axis, 1)} for axis in range(3)]
    down = [{names[axis]: lax.rem(here[axis] + sizes[axis] - 1, sizes[axis])} for axis in range(3)]

    barrier = pltpu.get_barrier_semaphore()
    for code in codes[1:]:
        pl.semaphore_signal(barrier, inc=1, device_id=device(code), device_id_type=MESH)

    middle, factors = step_factors()
    started = []

    def send(step, group, index, source, target, device_id):
        copy = pltpu.make_async_remote_copy(
            src_ref=source,
            dst_ref=target,
            send_sem=send_sem.at[step, group, index],
            recv_sem=recv_sem.at[step, group, index],
            device_id=device_id,
            device_id_type=MESH,
        )
        copy.start()
        started.append(copy)
        return copy

    def source_of(step):
        return orb_ref if step == 0 else field.at[step - 1]

    state = {}

    def send_faces(step, group):
        span = pl.ds(group * each, each)
        source = source_of(step)
        y_copies = [
            send(step, group, 2, source.at[span], y_in.at[step, 0, span], up[1])
        ]
        if size_y > 2:
            y_copies.append(send(step, group, 3, source.at[span], y_in.at[step, 1, span], down[1]))
        x_copies = [
            send(
                step, group, 0, source.at[span, pl.ds(cx - WIDTH, WIDTH)], x_low.at[step, span], up[0]
            ),
            send(step, group, 1, source.at[span, pl.ds(0, WIDTH)], x_high.at[step, span], down[0]),
        ]
        state[step, group] = {"x": x_copies, "y": y_copies}

    first = lax.broadcasted_iota(jnp.int32, (cz, cz), 0)
    second = lax.broadcasted_iota(jnp.int32, (cz, cz), 1)
    high, low = split_two(by_distance(first - second))
    band = jnp.concatenate(
        [
            jnp.concatenate([high, low], axis=1),
            jnp.concatenate([high, jnp.zeros_like(low)], axis=1),
        ],
        axis=0,
    )
    place = lax.broadcasted_iota(jnp.int32, (16, cz), 0)
    lane = lax.broadcasted_iota(jnp.int32, (16, cz), 1)
    high, low = split_two(by_distance(jnp.where(place < 8, place - 8, place - 8 + cz) - lane))
    edge_band = jnp.concatenate([high, high, low], axis=0)
    edge_pick = (lane == jnp.where(place < 8, place, place - 16 + cz)).astype(F32).astype(BF16)
    edge_pick = jnp.concatenate([edge_pick, edge_pick], axis=1)

    pl.semaphore_wait(barrier, blocks - 1)
    loads[0].wait()
    for group in range(groups):
        send_faces(0, group)

    for load in loads[1:]:
        load.wait()
    cells = cell_ref[...]
    lanes_of = cells % cz
    rows_of = cells // cz
    at_lane = (lax.broadcasted_iota(jnp.int32, (cz, points), 0) == lanes_of).astype(F32).astype(BF16)
    lane_hot[0:cz, :] = at_lane
    lane_hot[cz:2 * cz, :] = at_lane
    row_hot[...] = (lax.broadcasted_iota(jnp.int32, (rows, points), 0) == rows_of).astype(F32)
    owner = owner_ref[...]
    coords = (owner // (size_y * size_z), owner // size_z % size_y, owner % size_z)
    block = jnp.zeros_like(owner)
    for axis in range(3):
        remain = (coords[axis] - here[axis] + sizes[axis]) % sizes[axis]
        block = block * spans[axis] + jnp.minimum(remain, 2)
    segment = block * 8 + slot_ref[...]
    seg_hot[...] = (
        lax.broadcasted_iota(jnp.int32, (seg_rows, points), 0) == segment
    ).astype(F32).astype(BF16)
    live = lax.broadcasted_iota(jnp.int32, (nproj, points), 1) < count_ref[0]
    masked[...] = jnp.where(live, val_ref[...], 0.0)

    atoms = energy_ref.shape[1]
    domain = (here[0] * size_y + here[1]) * size_z + here[2]
    slots = lax.broadcasted_iota(jnp.int32, (8, atoms), 0)
    mine = (lax.broadcasted_iota(jnp.int32, (8, atoms), 1) == domain * ATOM_DEV + slots) & (
        slots < ATOM_DEV
    )
    lane_group = lax.broadcasted_iota(jnp.int32, (8, 128), 1) // each
    energies = jnp.zeros((8, 128), F32)
    for j in range(nproj):
        own = jnp.sum(jnp.where(mine, energy_ref[j:j + 1, :], 0.0), axis=1, keepdims=True)
        energies = jnp.where(lane_group == j, own, energies)

    used = nproj * each

    def begin(step, group):
        now = state[step, group]
        span = slice(group * each, group * each + each)
        flat = source_of(step)[span].reshape(each * rows, cz)
        high, low = split_two(flat)
        both = jnp.concatenate([high, low], axis=1)
        now["both"] = both
        z_out[step, group] = lax.dot_general(
            edge_pick, both, (((1,), (1,)), ((), ())), preferred_element_type=F32
        ).reshape(2, 8, each * rows)
        now["z"] = [
            send(step, group, 4, z_out.at[step, group, 1], z_in.at[step, group, 0], up[2]),
            send(step, group, 5, z_out.at[step, group, 0], z_in.at[step, group, 1], down[2]),
        ]
        weighted = []
        for start in range(0, points, CHUNK):
            part = slice(start, start + CHUNK)
            spread = jnp.dot(both, lane_hot[:, part], preferred_element_type=F32)
            sampled = jnp.sum(spread.reshape(each, rows, CHUNK) * row_hot[:, part][None], axis=1)
            weighted.append(
                jnp.concatenate([sampled * masked[j:j + 1, part] for j in range(nproj)], axis=0)
            )
        high, low = split_two(jnp.concatenate(weighted, axis=1))
        filler = jnp.zeros((128 - 2 * used, points), BF16)
        partial = lax.dot_general(
            seg_hot[...],
            jnp.concatenate([high, low, filler], axis=0),
            (((1,), (1,)), ((), ())),
            preferred_element_type=F32,
        )
        partial = partial + pltpu.roll(partial, 128 - used, 1)
        now["own"] = partial[0:8]
        part_out[step, group] = partial[0:blocks * 8].reshape(blocks, 8, 128)
        now["part"] = [
            send(
                step, group, 6 + n, part_out.at[step, group, n], part_in.at[step, group, n],
                device(codes[n]),
            )
            for n in range(1, blocks)
        ]

    def along_lanes(step, group):
        now = state[step, group]
        span = slice(group * each, group * each + each)
        total = jnp.dot(now["both"], band, preferred_element_type=F32)
        total = total[:, 0:cz] + total[:, cz:2 * cz]
        for copy in now["z"]:
            copy.wait_recv()
        high, low = split_two(z_in[step, group].reshape(16, each * rows))
        edges = jnp.concatenate([high.astype(F32), low.astype(F32), high.astype(F32)], axis=0)
        total = total + jnp.dot(edges.T.astype(BF16), edge_band, preferred_element_type=F32)
        acc[span] = total.reshape(each, cx, cy, cz)

    def give_back(step, group):
        now = state[step, group]
        owned = now["own"]
        for n, copy in enumerate(now["part"], 1):
            copy.wait_recv()
            owned = owned + part_in[step, group, n]
        coefficients = owned * energies
        now["own"] = coefficients
        coef_out[step, group] = coefficients
        now["coef"] = [
            send(
                step, group, 6 + blocks + n, coef_out.at[step, group],
                coef_in.at[step, group, opposite(codes[n])], device(codes[n]),
            )
            for n in range(1, blocks)
        ]

    def across_rows(step, group):
        now = state[step, group]
        for copy in now["x"] + now["y"]:
            copy.wait_recv()
        source = source_of(step)
        for o in range(group * each, group * each + each):
            own = source[o]
            total = acc[o] + (pot_ref[...] + (-1.5 * stencil_terms[0] - middle)) * own
            below = y_in[step, 0, o]
            above = below if size_y == 2 else y_in[step, 1, o]
            in_x = jnp.concatenate([x_low[step, o], own, x_high[step, o]], axis=0)
            in_y = jnp.concatenate([below, own, above], axis=1)
            for k in range(1, WIDTH + 1):
                total = total + (-0.5 * stencil_terms[k]) * (
                    (in_x[WIDTH + k:WIDTH + k + cx] + in_x[WIDTH - k:WIDTH - k + cx])
                    + (in_y[:, cy + k:2 * cy + k] + in_y[:, cy - k:2 * cy - k])
                )
            acc[o] = total

    def finish(step, group):
        now = state[step, group]
        for copy in now["coef"]:
            copy.wait_recv()
        around = jnp.concatenate(
            [now["own"]]
            + [coef_in[step, group, n] for n in range(1, blocks)]
            + [jnp.zeros((seg_rows - 8 * blocks, 128), F32)],
            axis=0,
        )
        high, low = split_two(around.T[0:used])
        spread = jnp.dot(
            jnp.concatenate([high, low], axis=0), seg_hot[...], preferred_element_type=F32
        )
        spread = spread[0:used] + spread[used:2 * used]
        returned = spread[0:each] * masked[0:1, :]
        for j in range(1, nproj):
            returned = returned + spread[j * each:(j + 1) * each] * masked[j:j + 1, :]
        high, low = split_two(returned)
        high, low = high.astype(F32), low.astype(F32)
        scattered = jnp.zeros((each * rows, cz), F32)
        for start in range(0, points, CHUNK):
            part = slice(start, start + CHUNK)
            at_row = row_hot[:, part].astype(BF16).reshape(1, rows // 16, 16, CHUNK)
            for term in (high, low):
                wide = jnp.broadcast_to(term[:, None, part], (each, 16, CHUNK)).astype(BF16)
                spots = wide[:, None] * at_row
                scattered = scattered + lax.dot_general(
                    spots.reshape(each * rows, CHUNK),
                    lane_hot[0:cz, part],
                    (((1,), (1,)), ((), ())),
                    preferred_element_type=F32,
                )
        scattered = scattered.reshape(each, cx, cy, cz)
        scale, keep = factors[step]
        span = slice(group * each, group * each + each)
        result = scale * (acc[span] + scattered)
        if step > 0:
            result = result + keep * source_of(step - 1)[span]
        if step < DEGREE - 1:
            field[step, span] = result
        else:
            out_ref[span] = result

    everyone = range(groups)
    for group in everyone:
        begin(0, group)
    for step in range(DEGREE):
        for group in everyone:
            along_lanes(step, group)
            give_back(step, group)
        for group in everyone:
            across_rows(step, group)
            finish(step, group)
            if step < DEGREE - 1:
                send_faces(step + 1, group)
                begin(step + 1, group)

    for copy in started:
        copy.wait_send()


def body(sizes, orbitals, potential, proj_values, point_cell, point_owner, point_slot, point_count, atom_energy):
    norb, cx, cy, cz = orbitals.shape
    nproj, points = proj_values.shape
    rows = cx * cy
    blocks = 1
    for size in sizes:
        blocks = blocks * min(3, size)
    seg_rows = (8 * blocks + 127) // 128 * 128
    copies = 6 + 2 * blocks
    groups = GROUPS
    each_rows = norb // groups * rows
    vmem = pl.BlockSpec(memory_space=pltpu.VMEM)
    smem = pl.BlockSpec(memory_space=pltpu.SMEM)
    hbm = pl.BlockSpec(memory_space=pltpu.HBM)
    return pl.pallas_call(
        functools.partial(kernel, sizes, groups),
        out_shape=jax.ShapeDtypeStruct(orbitals.shape, F32),
        in_specs=[hbm] * 6 + [smem, hbm],
        out_specs=vmem,
        scratch_shapes=[
            pltpu.VMEM(orbitals.shape, F32),
            pltpu.VMEM(potential.shape, F32),
            pltpu.VMEM(proj_values.shape, F32),
            pltpu.VMEM((1, points), jnp.int32),
            pltpu.VMEM((1, points), jnp.int32),
            pltpu.VMEM((1, points), jnp.int32),
            pltpu.VMEM(atom_energy.shape, F32),
            pltpu.VMEM((DEGREE - 1, norb, cx, cy, cz), F32),
            pltpu.VMEM((norb, cx, cy, cz), F32),
            pltpu.VMEM((DEGREE, norb, WIDTH, cy, cz), F32),
            pltpu.VMEM((DEGREE, norb, WIDTH, cy, cz), F32),
            pltpu.VMEM((DEGREE, 1 if sizes[1] == 2 else 2, norb, cx, cy, cz), F32),
            pltpu.VMEM((DEGREE, groups, 2, 8, each_rows), F32),
            pltpu.VMEM((DEGREE, groups, 2, 8, each_rows), F32),
            pltpu.VMEM((DEGREE, groups, blocks, 8, 128), F32),
            pltpu.VMEM((DEGREE, groups, blocks, 8, 128), F32),
            pltpu.VMEM((DEGREE, groups, 8, 128), F32),
            pltpu.VMEM((DEGREE, groups, blocks, 8, 128), F32),
            pltpu.VMEM((2 * cz, points), BF16),
            pltpu.VMEM((rows, points), F32),
            pltpu.VMEM((seg_rows, points), BF16),
            pltpu.VMEM((nproj, points), F32),
            pltpu.SemaphoreType.DMA((7,)),
            pltpu.SemaphoreType.DMA((DEGREE, groups, copies)),
            pltpu.SemaphoreType.DMA((DEGREE, groups, copies)),
        ],
        compiler_params=pltpu.CompilerParams(
            collective_id=0, has_side_effects=True, vmem_limit_bytes=63 * 1024 * 1024
        ),
    )(
        orbitals,
        potential,
        proj_values,
        point_cell.reshape(1, points),
        point_owner.reshape(1, points),
        point_slot.reshape(1, points),
        point_count,
        atom_energy,
    )


def solution(mesh):
    sizes = tuple(mesh.shape[name] for name in ("gx", "gy", "gz"))
    return jax.shard_map(
        functools.partial(body, sizes),
        mesh=mesh,
        in_specs=(
            P(None, "gx", "gy", "gz"),
            P("gx", "gy", "gz"),
            P(None, ("gx", "gy", "gz")),
            P(("gx", "gy", "gz")),
            P(("gx", "gy", "gz")),
            P(("gx", "gy", "gz")),
            P(("gx", "gy", "gz")),
            P(),
        ),
        out_specs=P(None, "gx", "gy", "gz"),
        check_vma=False,
    )
```

```python
import functools

import jax
import jax.numpy as jnp
from jax import lax
from jax.experimental import pallas as pl
from jax.experimental.pallas import tpu as pltpu
from jax.sharding import PartitionSpec as P

DEGREE = 3
ATOM_DEV = 5
WIDTH = 6
CHUNK = 256
GROUPS = 2
MESH = pl.DeviceIdType.MESH
F32 = jnp.float32
BF16 = jnp.bfloat16

stencil_terms = (
    -5369.0 / 1800.0,
    12.0 / 7.0,
    -15.0 / 56.0,
    10.0 / 189.0,
    -1.0 / 112.0,
    2.0 / 1925.0,
    -1.0 / 16632.0,
)
lowest = -3.5
cutoff = 1.5
highest = 13.0


def step_factors():
    half = (highest - cutoff) / 2.0
    middle = (highest + cutoff) / 2.0
    first = half / (lowest - middle)
    factors = [(first / half, 0.0)]
    sigma = first
    for _ in range(1, DEGREE):
        following = 1.0 / (2.0 / first - sigma)
        factors.append((2.0 * following / half, -sigma * following))
        sigma = following
    return middle, factors


def split_two(value):
    high = value.astype(BF16)
    low = (value - high.astype(F32)).astype(BF16)
    return high, low


def divided(value, by):
    if by & (by - 1):
        return value // by, value % by
    return value >> (by.bit_length() - 1), value & (by - 1)


def by_distance(distance):
    result = jnp.zeros(distance.shape, F32)
    for offset in range(WIDTH + 1):
        weight = 0.0 if offset == 0 else -0.5 * stencil_terms[offset]
        result = jnp.where(jnp.abs(distance) == offset, weight, result)
    return result


def kernel(
    sizes, groups,
    orb_hbm, pot_hbm, val_hbm, cell_hbm, owner_hbm, slot_hbm, count_ref, energy_hbm,
    out_ref,
    orb_ref, pot_ref, val_ref, cell_ref, owner_ref, slot_ref, energy_ref,
    field, acc, x_low, x_high, y_in, z_out, z_in, part_out, part_in, coef_out, coef_in,
    lane_hot, lane_turn, row_hot, seg_hot, seg_turn, masked, load_sem, send_sem, recv_sem,
):
    size_x, size_y, size_z = sizes
    norb, cx, cy, cz = orb_ref.shape
    nproj, points = val_ref.shape
    rows = cx * cy
    each = norb // groups
    spans = [min(3, size) for size in sizes]
    codes = [(a, b, c) for a in range(spans[0]) for b in range(spans[1]) for c in range(spans[2])]
    blocks = len(codes)
    seg_rows = seg_hot.shape[0]
    here = [lax.axis_index(name) for name in ("gx", "gy", "gz")]
    names = ("gx", "gy", "gz")

    loads = [
        pltpu.make_async_copy(source, target, load_sem.at[n])
        for n, (source, target) in enumerate(
            [
                (orb_hbm, orb_ref),
                (cell_hbm, cell_ref),
                (owner_hbm, owner_ref),
                (slot_hbm, slot_ref),
                (val_hbm, val_ref),
                (energy_hbm, energy_ref),
                (pot_hbm, pot_ref),
            ]
        )
    ]
    for load in loads:
        load.start()

    def moved(axis, code):
        step = (0, 1, sizes[axis] - 1)[code]
        return lax.rem(here[axis] + step, sizes[axis])

    def device(code):
        return {name: moved(axis, code[axis]) for axis, name in enumerate(names)}

    def opposite(code):
        back = [0 if c == 0 else (1 if sizes[a] == 2 else 3 - c) for a, c in enumerate(code)]
        return codes.index(tuple(back))

    up = [{names[axis]: moved(axis, 1)} for axis in range(3)]
    down = [{names[axis]: lax.rem(here[axis] + sizes[axis] - 1, sizes[axis])} for axis in range(3)]

    barrier = pltpu.get_barrier_semaphore()
    for code in codes[1:]:
        pl.semaphore_signal(barrier, inc=1, device_id=device(code), device_id_type=MESH)

    middle, factors = step_factors()
    started = []

    def send(step, group, index, source, target, device_id):
        copy = pltpu.make_async_remote_copy(
            src_ref=source,
            dst_ref=target,
            send_sem=send_sem.at[step, group, index],
            recv_sem=recv_sem.at[step, group, index],
            device_id=device_id,
            device_id_type=MESH,
        )
        copy.start()
        started.append(copy)
        return copy

    def source_of(step):
        return orb_ref if step == 0 else field.at[step - 1]

    state = {}

    def send_faces(step, group):
        span = pl.ds(group * each, each)
        source = source_of(step)
        y_copies = [
            send(step, group, 2, source.at[span], y_in.at[step, 0, span], up[1])
        ]
        if size_y > 2:
            y_copies.append(send(step, group, 3, source.at[span], y_in.at[step, 1, span], down[1]))
        x_copies = [
            send(
                step, group, 0, source.at[span, pl.ds(cx - WIDTH, WIDTH)], x_low.at[step, span], up[0]
            ),
            send(step, group, 1, source.at[span, pl.ds(0, WIDTH)], x_high.at[step, span], down[0]),
        ]
        state[step, group] = {"x": x_copies, "y": y_copies}

    first = lax.broadcasted_iota(jnp.int32, (cz, cz), 0)
    second = lax.broadcasted_iota(jnp.int32, (cz, cz), 1)
    high, low = split_two(by_distance(first - second))
    band = jnp.concatenate(
        [
            jnp.concatenate([high, low], axis=1),
            jnp.concatenate([high, jnp.zeros_like(low)], axis=1),
        ],
        axis=0,
    )
    place = lax.broadcasted_iota(jnp.int32, (16, cz), 0)
    lane = lax.broadcasted_iota(jnp.int32, (16, cz), 1)
    high, low = split_two(by_distance(jnp.where(place < 8, place - 8, place - 8 + cz) - lane))
    edge_band = jnp.concatenate([high, high, low], axis=0)
    edge_pick = (lane == jnp.where(place < 8, place, place - 16 + cz)).astype(F32).astype(BF16)
    edge_pick = jnp.concatenate([edge_pick, edge_pick], axis=1)

    pl.semaphore_wait(barrier, blocks - 1)
    loads[0].wait()
    for group in range(groups):
        send_faces(0, group)

    for load in loads[1:]:
        load.wait()
    cells = cell_ref[...]
    rows_of, lanes_of = divided(cells, cz)
    at_lane = (lax.broadcasted_iota(jnp.int32, (cz, points), 0) == lanes_of).astype(F32)
    lane_hot[0:cz, :] = at_lane.astype(BF16)
    lane_hot[cz:2 * cz, :] = at_lane.astype(BF16)
    lane_turn[...] = at_lane.T.astype(BF16)
    row_hot[...] = (lax.broadcasted_iota(jnp.int32, (rows, points), 0) == rows_of).astype(F32)
    owner = owner_ref[...]
    owner_xy, owner_z = divided(owner, size_z)
    owner_x, owner_y = divided(owner_xy, size_y)
    coords = (owner_x, owner_y, owner_z)
    block = jnp.zeros_like(owner)
    for axis in range(3):
        remain = divided(coords[axis] - here[axis] + sizes[axis], sizes[axis])[1]
        block = block * spans[axis] + jnp.minimum(remain, 2)
    segment = block * 8 + slot_ref[...]
    at_seg = (lax.broadcasted_iota(jnp.int32, (seg_rows, points), 0) == segment).astype(F32)
    seg_hot[...] = at_seg.astype(BF16)
    seg_turn[...] = at_seg.T.astype(BF16)
    live = lax.broadcasted_iota(jnp.int32, (nproj, points), 1) < count_ref[0]
    masked[...] = jnp.where(live, val_ref[...], 0.0)

    atoms = energy_ref.shape[1]
    domain = (here[0] * size_y + here[1]) * size_z + here[2]
    slots = lax.broadcasted_iota(jnp.int32, (8, atoms), 0)
    mine = (lax.broadcasted_iota(jnp.int32, (8, atoms), 1) == domain * ATOM_DEV + slots) & (
        slots < ATOM_DEV
    )
    lane_group = lax.broadcasted_iota(jnp.int32, (8, 128), 1) // each
    energies = jnp.zeros((8, 128), F32)
    for j in range(nproj):
        own = jnp.sum(jnp.where(mine, energy_ref[j:j + 1, :], 0.0), axis=1, keepdims=True)
        energies = jnp.where(lane_group == j, own, energies)

    used = nproj * each

    def begin(step, group):
        now = state[step, group]
        span = slice(group * each, group * each + each)
        flat = source_of(step)[span].reshape(each * rows, cz)
        high, low = split_two(flat)
        both = jnp.concatenate([high, low], axis=1)
        now["both"] = both
        z_out[step, group] = lax.dot_general(
            edge_pick, both, (((1,), (1,)), ((), ())), preferred_element_type=F32
        ).reshape(2, 8, each * rows)
        now["z"] = [
            send(step, group, 4, z_out.at[step, group, 1], z_in.at[step, group, 0], up[2]),
            send(step, group, 5, z_out.at[step, group, 0], z_in.at[step, group, 1], down[2]),
        ]
        weighted = []
        for start in range(0, points, CHUNK):
            part = slice(start, start + CHUNK)
            spread = jnp.dot(both, lane_hot[:, part], preferred_element_type=F32)
            sampled = jnp.sum(spread.reshape(each, rows, CHUNK) * row_hot[:, part][None], axis=1)
            weighted.append(
                jnp.concatenate([sampled * masked[j:j + 1, part] for j in range(nproj)], axis=0)
            )
        high, low = split_two(jnp.concatenate(weighted, axis=1))
        partial = jnp.dot(
            jnp.concatenate([high, low], axis=0), seg_turn[...], preferred_element_type=F32
        )
        partial = jnp.concatenate(
            [partial[0:used] + partial[used:2 * used], jnp.zeros((128 - used, seg_rows), F32)], axis=0
        ).T
        now["own"] = partial[0:8]
        part_out[step, group] = partial[0:blocks * 8].reshape(blocks, 8, 128)
        now["part"] = [
            send(
                step, group, 6 + n, part_out.at[step, group, n], part_in.at[step, group, n],
                device(codes[n]),
            )
            for n in range(1, blocks)
        ]

    def along_lanes(step, group):
        now = state[step, group]
        span = slice(group * each, group * each + each)
        total = jnp.dot(now["both"], band, preferred_element_type=F32)
        total = total[:, 0:cz] + total[:, cz:2 * cz]
        for copy in now["z"]:
            copy.wait_recv()
        high, low = split_two(z_in[step, group].reshape(16, each * rows))
        edges = jnp.concatenate([high.astype(F32), low.astype(F32), high.astype(F32)], axis=0)
        total = total + jnp.dot(edges.T.astype(BF16), edge_band, preferred_element_type=F32)
        acc[span] = total.reshape(each, cx, cy, cz)

    def give_back(step, group):
        now = state[step, group]
        owned = now["own"]
        for n, copy in enumerate(now["part"], 1):
            copy.wait_recv()
            owned = owned + part_in[step, group, n]
        coefficients = owned * energies
        now["own"] = coefficients
        coef_out[step, group] = coefficients
        now["coef"] = [
            send(
                step, group, 6 + blocks + n, coef_out.at[step, group],
                coef_in.at[step, group, opposite(codes[n])], device(codes[n]),
            )
            for n in range(1, blocks)
        ]

    def across_rows(step, group):
        now = state[step, group]
        for copy in now["x"] + now["y"]:
            copy.wait_recv()
        source = source_of(step)
        for o in range(group * each, group * each + each):
            own = source[o]
            total = acc[o] + (pot_ref[...] + (-1.5 * stencil_terms[0] - middle)) * own
            below = y_in[step, 0, o]
            above = below if size_y == 2 else y_in[step, 1, o]
            in_x = jnp.concatenate([x_low[step, o], own, x_high[step, o]], axis=0)
            in_y = jnp.concatenate([below, own, above], axis=1)
            for k in range(1, WIDTH + 1):
                total = total + (-0.5 * stencil_terms[k]) * (
                    (in_x[WIDTH + k:WIDTH + k + cx] + in_x[WIDTH - k:WIDTH - k + cx])
                    + (in_y[:, cy + k:2 * cy + k] + in_y[:, cy - k:2 * cy - k])
                )
            acc[o] = total

    def finish(step, group):
        now = state[step, group]
        for copy in now["coef"]:
            copy.wait_recv()
        around = jnp.concatenate(
            [now["own"]]
            + [coef_in[step, group, n] for n in range(1, blocks)]
            + [jnp.zeros((seg_rows - 8 * blocks, 128), F32)],
            axis=0,
        )
        high, low = split_two(around.T[0:used])
        spread = jnp.dot(
            jnp.concatenate([high, low], axis=0), seg_hot[...], preferred_element_type=F32
        )
        spread = spread[0:used] + spread[used:2 * used]
        returned = spread[0:each] * masked[0:1, :]
        for j in range(1, nproj):
            returned = returned + spread[j * each:(j + 1) * each] * masked[j:j + 1, :]
        high, low = split_two(returned)
        high, low = high.astype(F32), low.astype(F32)
        scattered = jnp.zeros((each * rows, cz), F32)
        for start in range(0, points, CHUNK):
            part = slice(start, start + CHUNK)
            at_row = row_hot[:, part].astype(BF16).reshape(1, rows // 16, 16, CHUNK)
            spots = []
            for term in (high, low):
                wide = jnp.broadcast_to(term[:, None, part], (each, 16, CHUNK)).astype(BF16)
                spots.append((wide[:, None] * at_row).reshape(each * rows, CHUNK))
            turned = lane_turn[part]
            scattered = scattered + jnp.dot(
                jnp.concatenate(spots, axis=1),
                jnp.concatenate([turned, turned], axis=0),
                preferred_element_type=F32,
            )
        scattered = scattered.reshape(each, cx, cy, cz)
        scale, keep = factors[step]
        span = slice(group * each, group * each + each)
        result = scale * (acc[span] + scattered)
        if step > 0:
            result = result + keep * source_of(step - 1)[span]
        if step < DEGREE - 1:
            field[step, span] = result
        else:
            out_ref[span] = result

    everyone = range(groups)
    for group in everyone:
        begin(0, group)
    for step in range(DEGREE):
        for group in everyone:
            along_lanes(step, group)
            give_back(step, group)
        for group in everyone:
            across_rows(step, group)
            finish(step, group)
            if step < DEGREE - 1:
                send_faces(step + 1, group)
                begin(step + 1, group)

    for copy in started:
        copy.wait_send()


def body(sizes, orbitals, potential, proj_values, point_cell, point_owner, point_slot, point_count, atom_energy):
    norb, cx, cy, cz = orbitals.shape
    nproj, points = proj_values.shape
    rows = cx * cy
    blocks = 1
    for size in sizes:
        blocks = blocks * min(3, size)
    seg_rows = (8 * blocks + 127) // 128 * 128
    copies = 6 + 2 * blocks
    groups = GROUPS
    each_rows = norb // groups * rows
    vmem = pl.BlockSpec(memory_space=pltpu.VMEM)
    smem = pl.BlockSpec(memory_space=pltpu.SMEM)
    hbm = pl.BlockSpec(memory_space=pltpu.HBM)
    return pl.pallas_call(
        functools.partial(kernel, sizes, groups),
        out_shape=jax.ShapeDtypeStruct(orbitals.shape, F32),
        in_specs=[hbm] * 6 + [smem, hbm],
        out_specs=vmem,
        scratch_shapes=[
            pltpu.VMEM(orbitals.shape, F32),
            pltpu.VMEM(potential.shape, F32),
            pltpu.VMEM(proj_values.shape, F32),
            pltpu.VMEM((1, points), jnp.int32),
            pltpu.VMEM((1, points), jnp.int32),
            pltpu.VMEM((1, points), jnp.int32),
            pltpu.VMEM(atom_energy.shape, F32),
            pltpu.VMEM((DEGREE - 1, norb, cx, cy, cz), F32),
            pltpu.VMEM((norb, cx, cy, cz), F32),
            pltpu.VMEM((DEGREE, norb, WIDTH, cy, cz), F32),
            pltpu.VMEM((DEGREE, norb, WIDTH, cy, cz), F32),
            pltpu.VMEM((DEGREE, 1 if sizes[1] == 2 else 2, norb, cx, cy, cz), F32),
            pltpu.VMEM((DEGREE, groups, 2, 8, each_rows), F32),
            pltpu.VMEM((DEGREE, groups, 2, 8, each_rows), F32),
            pltpu.VMEM((DEGREE, groups, blocks, 8, 128), F32),
            pltpu.VMEM((DEGREE, groups, blocks, 8, 128), F32),
            pltpu.VMEM((DEGREE, groups, 8, 128), F32),
            pltpu.VMEM((DEGREE, groups, blocks, 8, 128), F32),
            pltpu.VMEM((2 * cz, points), BF16),
            pltpu.VMEM((points, cz), BF16),
            pltpu.VMEM((rows, points), F32),
            pltpu.VMEM((seg_rows, points), BF16),
            pltpu.VMEM((points, seg_rows), BF16),
            pltpu.VMEM((nproj, points), F32),
            pltpu.SemaphoreType.DMA((7,)),
            pltpu.SemaphoreType.DMA((DEGREE, groups, copies)),
            pltpu.SemaphoreType.DMA((DEGREE, groups, copies)),
        ],
        compiler_params=pltpu.CompilerParams(
            collective_id=0, has_side_effects=True, vmem_limit_bytes=63 * 1024 * 1024
        ),
    )(
        orbitals,
        potential,
        proj_values,
        point_cell.reshape(1, points),
        point_owner.reshape(1, points),
        point_slot.reshape(1, points),
        point_count,
        atom_energy,
    )


def solution(mesh):
    sizes = tuple(mesh.shape[name] for name in ("gx", "gy", "gz"))
    return jax.shard_map(
        functools.partial(body, sizes),
        mesh=mesh,
        in_specs=(
            P(None, "gx", "gy", "gz"),
            P("gx", "gy", "gz"),
            P(None, ("gx", "gy", "gz")),
            P(("gx", "gy", "gz")),
            P(("gx", "gy", "gz")),
            P(("gx", "gy", "gz")),
            P(("gx", "gy", "gz")),
            P(),
        ),
        out_specs=P(None, "gx", "gy", "gz"),
        check_vma=False,
    )
```

```python
import functools

import jax
import jax.numpy as jnp
from jax import lax
from jax.experimental import pallas as pl
from jax.experimental.pallas import tpu as pltpu
from jax.sharding import PartitionSpec as P

DEGREE = 3
ATOM_DEV = 5
WIDTH = 6
CHUNK = 256
GROUPS = 2
MESH = pl.DeviceIdType.MESH
F32 = jnp.float32
BF16 = jnp.bfloat16

stencil_terms = (
    -5369.0 / 1800.0,
    12.0 / 7.0,
    -15.0 / 56.0,
    10.0 / 189.0,
    -1.0 / 112.0,
    2.0 / 1925.0,
    -1.0 / 16632.0,
)
lowest = -3.5
cutoff = 1.5
highest = 13.0


def step_factors():
    half = (highest - cutoff) / 2.0
    middle = (highest + cutoff) / 2.0
    first = half / (lowest - middle)
    factors = [(first / half, 0.0)]
    sigma = first
    for _ in range(1, DEGREE):
        following = 1.0 / (2.0 / first - sigma)
        factors.append((2.0 * following / half, -sigma * following))
        sigma = following
    return middle, factors


def split_two(value):
    high = value.astype(BF16)
    low = (value - high.astype(F32)).astype(BF16)
    return high, low


def divided(value, by):
    if by & (by - 1):
        return value // by, value % by
    return value >> (by.bit_length() - 1), value & (by - 1)


def by_distance(distance):
    result = jnp.zeros(distance.shape, F32)
    for offset in range(WIDTH + 1):
        weight = 0.0 if offset == 0 else -0.5 * stencil_terms[offset]
        result = jnp.where(jnp.abs(distance) == offset, weight, result)
    return result


def kernel(
    sizes, groups,
    orb_hbm, pot_hbm, val_hbm, cell_hbm, owner_hbm, slot_hbm, count_ref, energy_hbm,
    out_hbm,
    orb_ref, pot_ref, val_ref, cell_ref, owner_ref, slot_ref, energy_ref,
    field, acc, x_low, x_high, y_in, z_out, z_in, part_out, part_in, coef_out, coef_in,
    lane_hot, lane_turn, row_hot, seg_hot, seg_turn, masked, load_sem, store_sem, send_sem, recv_sem,
):
    size_x, size_y, size_z = sizes
    norb, cx, cy, cz = orb_ref.shape
    nproj, points = val_ref.shape
    rows = cx * cy
    each = norb // groups
    spans = [min(3, size) for size in sizes]
    codes = [(a, b, c) for a in range(spans[0]) for b in range(spans[1]) for c in range(spans[2])]
    blocks = len(codes)
    seg_rows = seg_hot.shape[0]
    here = [lax.axis_index(name) for name in ("gx", "gy", "gz")]
    names = ("gx", "gy", "gz")

    loads = [
        pltpu.make_async_copy(source, target, load_sem.at[n])
        for n, (source, target) in enumerate(
            [
                (orb_hbm, orb_ref),
                (cell_hbm, cell_ref),
                (owner_hbm, owner_ref),
                (slot_hbm, slot_ref),
                (val_hbm, val_ref),
                (energy_hbm, energy_ref),
                (pot_hbm, pot_ref),
            ]
        )
    ]
    for load in loads:
        load.start()

    places = [
        [here[axis]] + [lax.rem(here[axis] + step, sizes[axis]) for step in (1, sizes[axis] - 1)]
        for axis in range(3)
    ]

    def moved(axis, code):
        return places[axis][code]

    def device(code):
        return {name: moved(axis, code[axis]) for axis, name in enumerate(names)}

    def opposite(code):
        back = [0 if c == 0 else (1 if sizes[a] == 2 else 3 - c) for a, c in enumerate(code)]
        return codes.index(tuple(back))

    up = [{names[axis]: moved(axis, 1)} for axis in range(3)]
    down = [{names[axis]: moved(axis, 2)} for axis in range(3)]

    barrier = pltpu.get_barrier_semaphore()
    for code in codes[1:]:
        pl.semaphore_signal(barrier, inc=1, device_id=device(code), device_id_type=MESH)

    middle, factors = step_factors()
    started = []
    stores = []

    def send(step, group, index, source, target, device_id):
        copy = pltpu.make_async_remote_copy(
            src_ref=source,
            dst_ref=target,
            send_sem=send_sem.at[step, group, index],
            recv_sem=recv_sem.at[step, group, index],
            device_id=device_id,
            device_id_type=MESH,
        )
        copy.start()
        if index < 6:
            started.append(copy)
        return copy

    def await_tiles(step, group, sems, index):
        tiles = part_in.at[step, group, pl.ds(1, blocks - 1)]
        pltpu.make_async_copy(tiles, tiles, sems.at[step, group, index]).wait()

    def source_of(step):
        return orb_ref if step == 0 else field.at[step - 1]

    state = {}

    def send_faces(step, group):
        span = pl.ds(group * each, each)
        source = source_of(step)
        y_copies = [
            send(step, group, 2, source.at[span], y_in.at[step, 0, span], up[1])
        ]
        if size_y > 2:
            y_copies.append(send(step, group, 3, source.at[span], y_in.at[step, 1, span], down[1]))
        x_copies = [
            send(
                step, group, 0, source.at[span, pl.ds(cx - WIDTH, WIDTH)], x_low.at[step, span], up[0]
            ),
            send(step, group, 1, source.at[span, pl.ds(0, WIDTH)], x_high.at[step, span], down[0]),
        ]
        state[step, group] = {"x": x_copies, "y": y_copies}

    first = lax.broadcasted_iota(jnp.int32, (cz, cz), 0)
    second = lax.broadcasted_iota(jnp.int32, (cz, cz), 1)
    high, low = split_two(by_distance(first - second))
    band = jnp.concatenate(
        [
            jnp.concatenate([high, low], axis=1),
            jnp.concatenate([high, jnp.zeros_like(low)], axis=1),
        ],
        axis=0,
    )
    place = lax.broadcasted_iota(jnp.int32, (16, cz), 0)
    lane = lax.broadcasted_iota(jnp.int32, (16, cz), 1)
    high, low = split_two(by_distance(jnp.where(place < 8, place - 8, place - 8 + cz) - lane))
    edge_band = jnp.concatenate([high, high, low], axis=0)
    edge_pick = (lane == jnp.where(place < 8, place, place - 16 + cz)).astype(F32).astype(BF16)
    edge_pick = jnp.concatenate([edge_pick, edge_pick], axis=1)

    pl.semaphore_wait(barrier, blocks - 1)
    loads[0].wait()
    for group in range(groups):
        send_faces(0, group)

    for load in loads[1:]:
        load.wait()
    cells = cell_ref[...]
    rows_of, lanes_of = divided(cells, cz)
    at_lane = (lax.broadcasted_iota(jnp.int32, (cz, points), 0) == lanes_of).astype(F32)
    lane_hot[0:cz, :] = at_lane.astype(BF16)
    lane_hot[cz:2 * cz, :] = at_lane.astype(BF16)
    lane_turn[...] = at_lane.T.astype(BF16)
    row_hot[...] = (lax.broadcasted_iota(jnp.int32, (rows, points), 0) == rows_of).astype(F32)
    owner = owner_ref[...]
    owner_xy, owner_z = divided(owner, size_z)
    owner_x, owner_y = divided(owner_xy, size_y)
    coords = (owner_x, owner_y, owner_z)
    block = jnp.zeros_like(owner)
    for axis in range(3):
        remain = divided(coords[axis] - here[axis] + sizes[axis], sizes[axis])[1]
        block = block * spans[axis] + jnp.minimum(remain, 2)
    segment = block * 8 + slot_ref[...]
    at_seg = (lax.broadcasted_iota(jnp.int32, (seg_rows, points), 0) == segment).astype(F32)
    seg_hot[...] = at_seg.astype(BF16)
    seg_turn[...] = at_seg.T.astype(BF16)
    live = lax.broadcasted_iota(jnp.int32, (nproj, points), 1) < count_ref[0]
    masked[...] = jnp.where(live, val_ref[...], 0.0)

    atoms = energy_ref.shape[1]
    domain = (here[0] * size_y + here[1]) * size_z + here[2]
    slots = lax.broadcasted_iota(jnp.int32, (8, atoms), 0)
    mine = (lax.broadcasted_iota(jnp.int32, (8, atoms), 1) == domain * ATOM_DEV + slots) & (
        slots < ATOM_DEV
    )
    lane_group = lax.broadcasted_iota(jnp.int32, (8, 128), 1) // each
    energies = jnp.zeros((8, 128), F32)
    for j in range(nproj):
        own = jnp.sum(jnp.where(mine, energy_ref[j:j + 1, :], 0.0), axis=1, keepdims=True)
        energies = jnp.where(lane_group == j, own, energies)

    used = nproj * each

    def begin(step, group):
        now = state[step, group]
        span = slice(group * each, group * each + each)
        flat = source_of(step)[span].reshape(each * rows, cz)
        high, low = split_two(flat)
        both = jnp.concatenate([high, low], axis=1)
        now["both"] = both
        z_out[step, group] = lax.dot_general(
            edge_pick, both, (((1,), (1,)), ((), ())), preferred_element_type=F32
        ).reshape(2, 8, each * rows)
        now["z"] = [
            send(step, group, 4, z_out.at[step, group, 1], z_in.at[step, group, 0], up[2]),
            send(step, group, 5, z_out.at[step, group, 0], z_in.at[step, group, 1], down[2]),
        ]
        weighted = []
        for start in range(0, points, CHUNK):
            part = slice(start, start + CHUNK)
            spread = jnp.dot(both, lane_hot[:, part], preferred_element_type=F32)
            sampled = jnp.sum(spread.reshape(each, rows, CHUNK) * row_hot[:, part][None], axis=1)
            weighted.append(
                jnp.concatenate([sampled * masked[j:j + 1, part] for j in range(nproj)], axis=0)
            )
        high, low = split_two(jnp.concatenate(weighted, axis=1))
        partial = jnp.dot(
            jnp.concatenate([high, low], axis=0), seg_turn[...], preferred_element_type=F32
        )
        partial = jnp.concatenate(
            [partial[0:used] + partial[used:2 * used], jnp.zeros((128 - used, seg_rows), F32)], axis=0
        ).T
        now["own"] = partial[0:8]
        part_out[step, group] = partial[0:blocks * 8].reshape(blocks, 8, 128)
        for n in range(1, blocks):
            send(
                step, group, 6, part_out.at[step, group, n], part_in.at[step, group, n],
                device(codes[n]),
            )

    def along_lanes(step, group):
        now = state[step, group]
        span = slice(group * each, group * each + each)
        total = jnp.dot(now["both"], band, preferred_element_type=F32)
        total = total[:, 0:cz] + total[:, cz:2 * cz]
        for copy in now["z"]:
            copy.wait_recv()
        high, low = split_two(z_in[step, group].reshape(16, each * rows))
        edges = jnp.concatenate([high.astype(F32), low.astype(F32), high.astype(F32)], axis=0)
        total = total + jnp.dot(edges.T.astype(BF16), edge_band, preferred_element_type=F32)
        acc[span] = total.reshape(each, cx, cy, cz)

    def give_back(step, group):
        now = state[step, group]
        owned = now["own"]
        await_tiles(step, group, recv_sem, 6)
        for n in range(1, blocks):
            owned = owned + part_in[step, group, n]
        coefficients = owned * energies
        now["own"] = coefficients
        coef_out[step, group] = coefficients
        for n in range(1, blocks):
            send(
                step, group, 7, coef_out.at[step, group],
                coef_in.at[step, group, opposite(codes[n])], device(codes[n]),
            )

    def across_rows(step, group):
        now = state[step, group]
        for copy in now["x"] + now["y"]:
            copy.wait_recv()
        source = source_of(step)
        for o in range(group * each, group * each + each):
            own = source[o]
            total = acc[o] + (pot_ref[...] + (-1.5 * stencil_terms[0] - middle)) * own
            below = y_in[step, 0, o]
            above = below if size_y == 2 else y_in[step, 1, o]
            in_x = jnp.concatenate([x_low[step, o], own, x_high[step, o]], axis=0)
            in_y = jnp.concatenate([below, own, above], axis=1)
            for k in range(1, WIDTH + 1):
                total = total + (-0.5 * stencil_terms[k]) * (
                    (in_x[WIDTH + k:WIDTH + k + cx] + in_x[WIDTH - k:WIDTH - k + cx])
                    + (in_y[:, cy + k:2 * cy + k] + in_y[:, cy - k:2 * cy - k])
                )
            acc[o] = total

    def finish(step, group):
        now = state[step, group]
        coefs = coef_in.at[step, group, pl.ds(1, blocks - 1)]
        pltpu.make_async_copy(coefs, coefs, recv_sem.at[step, group, 7]).wait()
        around = jnp.concatenate(
            [now["own"]]
            + [coef_in[step, group, n] for n in range(1, blocks)]
            + [jnp.zeros((seg_rows - 8 * blocks, 128), F32)],
            axis=0,
        )
        high, low = split_two(around.T[0:used])
        spread = jnp.dot(
            jnp.concatenate([high, low], axis=0), seg_hot[...], preferred_element_type=F32
        )
        spread = spread[0:used] + spread[used:2 * used]
        returned = spread[0:each] * masked[0:1, :]
        for j in range(1, nproj):
            returned = returned + spread[j * each:(j + 1) * each] * masked[j:j + 1, :]
        high, low = split_two(returned)
        high, low = high.astype(F32), low.astype(F32)
        scattered = jnp.zeros((each * rows, cz), F32)
        for start in range(0, points, CHUNK):
            part = slice(start, start + CHUNK)
            at_row = row_hot[:, part].astype(BF16).reshape(1, rows // 16, 16, CHUNK)
            spots = []
            for term in (high, low):
                wide = jnp.broadcast_to(term[:, None, part], (each, 16, CHUNK)).astype(BF16)
                spots.append((wide[:, None] * at_row).reshape(each * rows, CHUNK))
            turned = lane_turn[part]
            scattered = scattered + jnp.dot(
                jnp.concatenate(spots, axis=1),
                jnp.concatenate([turned, turned], axis=0),
                preferred_element_type=F32,
            )
        scattered = scattered.reshape(each, cx, cy, cz)
        scale, keep = factors[step]
        span = slice(group * each, group * each + each)
        result = scale * (acc[span] + scattered)
        if step > 0:
            result = result + keep * source_of(step - 1)[span]
        if step < DEGREE - 1:
            field[step, span] = result
        else:
            acc[span] = result
            stores.append(
                pltpu.make_async_copy(acc.at[span], out_hbm.at[span], store_sem.at[group])
            )
            stores[-1].start()

    everyone = range(groups)
    for group in everyone:
        begin(0, group)
    for step in range(DEGREE):
        for group in everyone:
            along_lanes(step, group)
            give_back(step, group)
        for group in everyone:
            across_rows(step, group)
            finish(step, group)
            if step < DEGREE - 1:
                send_faces(step + 1, group)
                begin(step + 1, group)

    for copy in started:
        copy.wait_send()
    for step in range(DEGREE):
        for group in everyone:
            await_tiles(step, group, send_sem, 6)
            await_tiles(step, group, send_sem, 7)
    for store in stores:
        store.wait()


def body(sizes, orbitals, potential, proj_values, point_cell, point_owner, point_slot, point_count, atom_energy):
    norb, cx, cy, cz = orbitals.shape
    nproj, points = proj_values.shape
    rows = cx * cy
    blocks = 1
    for size in sizes:
        blocks = blocks * min(3, size)
    seg_rows = (8 * blocks + 127) // 128 * 128
    copies = 8
    groups = GROUPS
    each_rows = norb // groups * rows
    smem = pl.BlockSpec(memory_space=pltpu.SMEM)
    hbm = pl.BlockSpec(memory_space=pltpu.HBM)
    return pl.pallas_call(
        functools.partial(kernel, sizes, groups),
        out_shape=jax.ShapeDtypeStruct(orbitals.shape, F32),
        in_specs=[hbm] * 6 + [smem, hbm],
        out_specs=hbm,
        scratch_shapes=[
            pltpu.VMEM(orbitals.shape, F32),
            pltpu.VMEM(potential.shape, F32),
            pltpu.VMEM(proj_values.shape, F32),
            pltpu.VMEM((1, points), jnp.int32),
            pltpu.VMEM((1, points), jnp.int32),
            pltpu.VMEM((1, points), jnp.int32),
            pltpu.VMEM(atom_energy.shape, F32),
            pltpu.VMEM((DEGREE - 1, norb, cx, cy, cz), F32),
            pltpu.VMEM((norb, cx, cy, cz), F32),
            pltpu.VMEM((DEGREE, norb, WIDTH, cy, cz), F32),
            pltpu.VMEM((DEGREE, norb, WIDTH, cy, cz), F32),
            pltpu.VMEM((DEGREE, 1 if sizes[1] == 2 else 2, norb, cx, cy, cz), F32),
            pltpu.VMEM((DEGREE, groups, 2, 8, each_rows), F32),
            pltpu.VMEM((DEGREE, groups, 2, 8, each_rows), F32),
            pltpu.VMEM((DEGREE, groups, blocks, 8, 128), F32),
            pltpu.VMEM((DEGREE, groups, blocks, 8, 128), F32),
            pltpu.VMEM((DEGREE, groups, 8, 128), F32),
            pltpu.VMEM((DEGREE, groups, blocks, 8, 128), F32),
            pltpu.VMEM((2 * cz, points), BF16),
            pltpu.VMEM((points, cz), BF16),
            pltpu.VMEM((rows, points), F32),
            pltpu.VMEM((seg_rows, points), BF16),
            pltpu.VMEM((points, seg_rows), BF16),
            pltpu.VMEM((nproj, points), F32),
            pltpu.SemaphoreType.DMA((7,)),
            pltpu.SemaphoreType.DMA((groups,)),
            pltpu.SemaphoreType.DMA((DEGREE, groups, copies)),
            pltpu.SemaphoreType.DMA((DEGREE, groups, copies)),
        ],
        compiler_params=pltpu.CompilerParams(
            collective_id=0, has_side_effects=True, vmem_limit_bytes=63 * 1024 * 1024
        ),
    )(
        orbitals,
        potential,
        proj_values,
        point_cell.reshape(1, points),
        point_owner.reshape(1, points),
        point_slot.reshape(1, points),
        point_count,
        atom_energy,
    )


def solution(mesh):
    sizes = tuple(mesh.shape[name] for name in ("gx", "gy", "gz"))
    return jax.shard_map(
        functools.partial(body, sizes),
        mesh=mesh,
        in_specs=(
            P(None, "gx", "gy", "gz"),
            P("gx", "gy", "gz"),
            P(None, ("gx", "gy", "gz")),
            P(("gx", "gy", "gz")),
            P(("gx", "gy", "gz")),
            P(("gx", "gy", "gz")),
            P(("gx", "gy", "gz")),
            P(),
        ),
        out_specs=P(None, "gx", "gy", "gz"),
        check_vma=False,
    )
```

```python
import functools

import jax
import jax.numpy as jnp
from jax import lax
from jax.experimental import pallas as pl
from jax.experimental.pallas import tpu as pltpu
from jax.sharding import PartitionSpec as P

DEGREE = 3
ATOM_DEV = 5
WIDTH = 6
CHUNK = 256
GROUPS = 2
MESH = pl.DeviceIdType.MESH
F32 = jnp.float32
BF16 = jnp.bfloat16

stencil_terms = (
    -5369.0 / 1800.0,
    12.0 / 7.0,
    -15.0 / 56.0,
    10.0 / 189.0,
    -1.0 / 112.0,
    2.0 / 1925.0,
    -1.0 / 16632.0,
)
lowest = -3.5
cutoff = 1.5
highest = 13.0


def step_factors():
    half = (highest - cutoff) / 2.0
    middle = (highest + cutoff) / 2.0
    first = half / (lowest - middle)
    factors = [(first / half, 0.0)]
    sigma = first
    for _ in range(1, DEGREE):
        following = 1.0 / (2.0 / first - sigma)
        factors.append((2.0 * following / half, -sigma * following))
        sigma = following
    return middle, factors


def split_two(value):
    high = value.astype(BF16)
    low = (value - high.astype(F32)).astype(BF16)
    return high, low


def divided(value, by):
    if by & (by - 1):
        return value // by, value % by
    return value >> (by.bit_length() - 1), value & (by - 1)


def by_distance(distance):
    result = jnp.zeros(distance.shape, F32)
    for offset in range(WIDTH + 1):
        weight = 0.0 if offset == 0 else -0.5 * stencil_terms[offset]
        result = jnp.where(jnp.abs(distance) == offset, weight, result)
    return result


def kernel(
    sizes, groups,
    orb_hbm, pot_hbm, val_hbm, cell_hbm, owner_hbm, slot_hbm, count_ref, energy_hbm,
    out_hbm,
    orb_ref, pot_ref, val_ref, cell_ref, owner_ref, slot_ref, energy_ref,
    field, acc, x_low, x_high, y_in, z_out, z_in, part_out, part_in, coef_out, coef_in,
    lane_hot, lane_turn, row_hot, seg_hot, seg_turn, masked, packed, around, load_sem, store_sem, send_sem, recv_sem,
):
    size_x, size_y, size_z = sizes
    norb, cx, cy, cz = orb_ref.shape
    nproj, points = val_ref.shape
    rows = cx * cy
    each = norb // groups
    spans = [min(3, size) for size in sizes]
    codes = [(a, b, c) for a in range(spans[0]) for b in range(spans[1]) for c in range(spans[2])]
    blocks = len(codes)
    seg_rows = seg_hot.shape[0]
    here = [lax.axis_index(name) for name in ("gx", "gy", "gz")]
    names = ("gx", "gy", "gz")

    loads = [
        pltpu.make_async_copy(source, target, load_sem.at[n])
        for n, (source, target) in enumerate(
            [
                (orb_hbm, orb_ref),
                (cell_hbm, cell_ref),
                (owner_hbm, owner_ref),
                (slot_hbm, slot_ref),
                (val_hbm, val_ref),
                (energy_hbm, energy_ref),
                (pot_hbm, pot_ref),
            ]
        )
    ]
    for load in loads:
        load.start()

    places = [
        [here[axis]] + [lax.rem(here[axis] + step, sizes[axis]) for step in (1, sizes[axis] - 1)]
        for axis in range(3)
    ]

    def moved(axis, code):
        return places[axis][code]

    def device(code):
        return {name: moved(axis, code[axis]) for axis, name in enumerate(names)}

    def opposite(code):
        back = [0 if c == 0 else (1 if sizes[a] == 2 else 3 - c) for a, c in enumerate(code)]
        return codes.index(tuple(back))

    up = [{names[axis]: moved(axis, 1)} for axis in range(3)]
    down = [{names[axis]: moved(axis, 2)} for axis in range(3)]

    barrier = pltpu.get_barrier_semaphore()
    for code in codes[1:]:
        pl.semaphore_signal(barrier, inc=1, device_id=device(code), device_id_type=MESH)

    middle, factors = step_factors()
    started = []
    stores = []

    def send(step, group, index, source, target, device_id):
        copy = pltpu.make_async_remote_copy(
            src_ref=source,
            dst_ref=target,
            send_sem=send_sem.at[step, group, index],
            recv_sem=recv_sem.at[step, group, index],
            device_id=device_id,
            device_id_type=MESH,
        )
        copy.start()
        if index < 6:
            started.append(copy)
        return copy

    def await_tiles(step, group, sems, index):
        tiles = part_in.at[step, group, pl.ds(1, blocks - 1)]
        pltpu.make_async_copy(tiles, tiles, sems.at[step, group, index]).wait()

    def source_of(step):
        return orb_ref if step == 0 else field.at[step - 1]

    state = {}

    def send_faces(step, group):
        span = pl.ds(group * each, each)
        source = source_of(step)
        y_copies = [
            send(step, group, 2, source.at[span], y_in.at[step, 0, span], up[1])
        ]
        if size_y > 2:
            y_copies.append(send(step, group, 3, source.at[span], y_in.at[step, 1, span], down[1]))
        x_copies = [
            send(
                step, group, 0, source.at[span, pl.ds(cx - WIDTH, WIDTH)], x_low.at[step, span], up[0]
            ),
            send(step, group, 1, source.at[span, pl.ds(0, WIDTH)], x_high.at[step, span], down[0]),
        ]
        state[step, group] = {"x": x_copies, "y": y_copies}

    first = lax.broadcasted_iota(jnp.int32, (cz, cz), 0)
    second = lax.broadcasted_iota(jnp.int32, (cz, cz), 1)
    high, low = split_two(by_distance(first - second))
    band = jnp.concatenate(
        [
            jnp.concatenate([high, low], axis=1),
            jnp.concatenate([high, jnp.zeros_like(low)], axis=1),
        ],
        axis=0,
    )
    place = lax.broadcasted_iota(jnp.int32, (16, cz), 0)
    lane = lax.broadcasted_iota(jnp.int32, (16, cz), 1)
    high, low = split_two(by_distance(jnp.where(place < 8, place - 8, place - 8 + cz) - lane))
    edge_band = jnp.concatenate([high, high, low], axis=0)
    edge_pick = (lane == jnp.where(place < 8, place, place - 16 + cz)).astype(F32).astype(BF16)
    edge_pick = jnp.concatenate([edge_pick, edge_pick], axis=1)

    pl.semaphore_wait(barrier, blocks - 1)
    loads[0].wait()
    for group in range(groups):
        send_faces(0, group)

    for load in loads[1:]:
        load.wait()
    cells = cell_ref[...]
    rows_of, lanes_of = divided(cells, cz)
    at_lane = (lax.broadcasted_iota(jnp.int32, (cz, points), 0) == lanes_of).astype(F32)
    lane_hot[0:cz, :] = at_lane.astype(BF16)
    lane_hot[cz:2 * cz, :] = at_lane.astype(BF16)
    lane_turn[...] = at_lane.T.astype(BF16)
    row_hot[...] = (lax.broadcasted_iota(jnp.int32, (rows, points), 0) == rows_of).astype(F32)
    owner = owner_ref[...]
    owner_xy, owner_z = divided(owner, size_z)
    owner_x, owner_y = divided(owner_xy, size_y)
    coords = (owner_x, owner_y, owner_z)
    block = jnp.zeros_like(owner)
    for axis in range(3):
        remain = divided(coords[axis] - here[axis] + sizes[axis], sizes[axis])[1]
        block = block * spans[axis] + jnp.minimum(remain, 2)
    segment = block * ATOM_DEV + slot_ref[...]
    at_seg = (lax.broadcasted_iota(jnp.int32, (seg_rows, points), 0) == segment).astype(F32)
    seg_hot[...] = at_seg.astype(BF16)
    seg_turn[...] = at_seg.T.astype(BF16)
    live = lax.broadcasted_iota(jnp.int32, (nproj, points), 1) < count_ref[0]
    masked[...] = jnp.where(live, val_ref[...], 0.0)

    atoms = energy_ref.shape[1]
    domain = (here[0] * size_y + here[1]) * size_z + here[2]
    slots = lax.broadcasted_iota(jnp.int32, (8, atoms), 0)
    mine = (lax.broadcasted_iota(jnp.int32, (8, atoms), 1) == domain * ATOM_DEV + slots) & (
        slots < ATOM_DEV
    )
    lane_group = lax.broadcasted_iota(jnp.int32, (8, 128), 1) // each
    energies = jnp.zeros((8, 128), F32)
    for j in range(nproj):
        own = jnp.sum(jnp.where(mine, energy_ref[j:j + 1, :], 0.0), axis=1, keepdims=True)
        energies = jnp.where(lane_group == j, own, energies)

    used = nproj * each
    around[...] = jnp.zeros(around.shape, F32)

    def begin(step, group):
        now = state[step, group]
        span = slice(group * each, group * each + each)
        flat = source_of(step)[span].reshape(each * rows, cz)
        high, low = split_two(flat)
        both = jnp.concatenate([high, low], axis=1)
        now["both"] = both
        z_out[step, group] = lax.dot_general(
            edge_pick, both, (((1,), (1,)), ((), ())), preferred_element_type=F32
        ).reshape(2, 8, each * rows)
        now["z"] = [
            send(step, group, 4, z_out.at[step, group, 1], z_in.at[step, group, 0], up[2]),
            send(step, group, 5, z_out.at[step, group, 0], z_in.at[step, group, 1], down[2]),
        ]
        weighted = []
        for start in range(0, points, CHUNK):
            part = slice(start, start + CHUNK)
            spread = jnp.dot(both, lane_hot[:, part], preferred_element_type=F32)
            sampled = jnp.sum(spread.reshape(each, rows, CHUNK) * row_hot[:, part][None], axis=1)
            weighted.append(
                jnp.concatenate([sampled * masked[j:j + 1, part] for j in range(nproj)], axis=0)
            )
        high, low = split_two(jnp.concatenate(weighted, axis=1))
        partial = jnp.dot(
            jnp.concatenate([high, low], axis=0), seg_turn[...], preferred_element_type=F32
        )
        partial = jnp.concatenate(
            [partial[0:used] + partial[used:2 * used], jnp.zeros((128 - used, seg_rows), F32)], axis=0
        ).T
        now["own"] = partial[0:8]
        packed[...] = partial
        for n in range(1, blocks):
            part_out[step, group, n] = packed[n * ATOM_DEV:n * ATOM_DEV + 8]
        for n in range(1, blocks):
            send(
                step, group, 6, part_out.at[step, group, n], part_in.at[step, group, n],
                device(codes[n]),
            )

    def along_lanes(step, group):
        now = state[step, group]
        span = slice(group * each, group * each + each)
        total = jnp.dot(now["both"], band, preferred_element_type=F32)
        total = total[:, 0:cz] + total[:, cz:2 * cz]
        for copy in now["z"]:
            copy.wait_recv()
        high, low = split_two(z_in[step, group].reshape(16, each * rows))
        edges = jnp.concatenate([high.astype(F32), low.astype(F32), high.astype(F32)], axis=0)
        total = total + jnp.dot(edges.T.astype(BF16), edge_band, preferred_element_type=F32)
        acc[span] = total.reshape(each, cx, cy, cz)

    def give_back(step, group):
        now = state[step, group]
        owned = now["own"]
        await_tiles(step, group, recv_sem, 6)
        for n in range(1, blocks):
            owned = owned + part_in[step, group, n]
        coefficients = owned * energies
        now["own"] = coefficients
        coef_out[step, group] = coefficients
        for n in range(1, blocks):
            send(
                step, group, 7, coef_out.at[step, group],
                coef_in.at[step, group, opposite(codes[n])], device(codes[n]),
            )

    def across_rows(step, group):
        now = state[step, group]
        for copy in now["x"] + now["y"]:
            copy.wait_recv()
        source = source_of(step)
        for o in range(group * each, group * each + each):
            own = source[o]
            total = acc[o] + (pot_ref[...] + (-1.5 * stencil_terms[0] - middle)) * own
            below = y_in[step, 0, o]
            above = below if size_y == 2 else y_in[step, 1, o]
            in_x = jnp.concatenate([x_low[step, o], own, x_high[step, o]], axis=0)
            in_y = jnp.concatenate([below, own, above], axis=1)
            for k in range(1, WIDTH + 1):
                total = total + (-0.5 * stencil_terms[k]) * (
                    (in_x[WIDTH + k:WIDTH + k + cx] + in_x[WIDTH - k:WIDTH - k + cx])
                    + (in_y[:, cy + k:2 * cy + k] + in_y[:, cy - k:2 * cy - k])
                )
            acc[o] = total

    def finish(step, group):
        now = state[step, group]
        coefs = coef_in.at[step, group, pl.ds(1, blocks - 1)]
        pltpu.make_async_copy(coefs, coefs, recv_sem.at[step, group, 7]).wait()
        around[0:8] = now["own"]
        for n in range(1, blocks):
            around[n * ATOM_DEV:n * ATOM_DEV + 8] = coef_in[step, group, n]
        high, low = split_two(around[...].T[0:used])
        spread = jnp.dot(
            jnp.concatenate([high, low], axis=0), seg_hot[...], preferred_element_type=F32
        )
        spread = spread[0:used] + spread[used:2 * used]
        returned = spread[0:each] * masked[0:1, :]
        for j in range(1, nproj):
            returned = returned + spread[j * each:(j + 1) * each] * masked[j:j + 1, :]
        high, low = split_two(returned)
        high, low = high.astype(F32), low.astype(F32)
        scattered = jnp.zeros((each * rows, cz), F32)
        for start in range(0, points, CHUNK):
            part = slice(start, start + CHUNK)
            at_row = row_hot[:, part].astype(BF16).reshape(1, rows // 16, 16, CHUNK)
            spots = []
            for term in (high, low):
                wide = jnp.broadcast_to(term[:, None, part], (each, 16, CHUNK)).astype(BF16)
                spots.append((wide[:, None] * at_row).reshape(each * rows, CHUNK))
            turned = lane_turn[part]
            scattered = scattered + jnp.dot(
                jnp.concatenate(spots, axis=1),
                jnp.concatenate([turned, turned], axis=0),
                preferred_element_type=F32,
            )
        scattered = scattered.reshape(each, cx, cy, cz)
        scale, keep = factors[step]
        span = slice(group * each, group * each + each)
        result = scale * (acc[span] + scattered)
        if step > 0:
            result = result + keep * source_of(step - 1)[span]
        if step < DEGREE - 1:
            field[step, span] = result
        else:
            acc[span] = result
            stores.append(
                pltpu.make_async_copy(acc.at[span], out_hbm.at[span], store_sem.at[group])
            )
            stores[-1].start()

    everyone = range(groups)
    for group in everyone:
        begin(0, group)
    for step in range(DEGREE):
        for group in everyone:
            along_lanes(step, group)
            give_back(step, group)
        for group in everyone:
            across_rows(step, group)
            finish(step, group)
            if step < DEGREE - 1:
                send_faces(step + 1, group)
                begin(step + 1, group)

    for copy in started:
        copy.wait_send()
    for step in range(DEGREE):
        for group in everyone:
            await_tiles(step, group, send_sem, 6)
            await_tiles(step, group, send_sem, 7)
    for store in stores:
        store.wait()


def body(sizes, orbitals, potential, proj_values, point_cell, point_owner, point_slot, point_count, atom_energy):
    norb, cx, cy, cz = orbitals.shape
    nproj, points = proj_values.shape
    rows = cx * cy
    blocks = 1
    for size in sizes:
        blocks = blocks * min(3, size)
    seg_rows = (ATOM_DEV * blocks + 8 + 127) // 128 * 128
    copies = 8
    groups = GROUPS
    each_rows = norb // groups * rows
    smem = pl.BlockSpec(memory_space=pltpu.SMEM)
    hbm = pl.BlockSpec(memory_space=pltpu.HBM)
    return pl.pallas_call(
        functools.partial(kernel, sizes, groups),
        out_shape=jax.ShapeDtypeStruct(orbitals.shape, F32),
        in_specs=[hbm] * 6 + [smem, hbm],
        out_specs=hbm,
        scratch_shapes=[
            pltpu.VMEM(orbitals.shape, F32),
            pltpu.VMEM(potential.shape, F32),
            pltpu.VMEM(proj_values.shape, F32),
            pltpu.VMEM((1, points), jnp.int32),
            pltpu.VMEM((1, points), jnp.int32),
            pltpu.VMEM((1, points), jnp.int32),
            pltpu.VMEM(atom_energy.shape, F32),
            pltpu.VMEM((DEGREE - 1, norb, cx, cy, cz), F32),
            pltpu.VMEM((norb, cx, cy, cz), F32),
            pltpu.VMEM((DEGREE, norb, WIDTH, cy, cz), F32),
            pltpu.VMEM((DEGREE, norb, WIDTH, cy, cz), F32),
            pltpu.VMEM((DEGREE, 1 if sizes[1] == 2 else 2, norb, cx, cy, cz), F32),
            pltpu.VMEM((DEGREE, groups, 2, 8, each_rows), F32),
            pltpu.VMEM((DEGREE, groups, 2, 8, each_rows), F32),
            pltpu.VMEM((DEGREE, groups, blocks, 8, 128), F32),
            pltpu.VMEM((DEGREE, groups, blocks, 8, 128), F32),
            pltpu.VMEM((DEGREE, groups, 8, 128), F32),
            pltpu.VMEM((DEGREE, groups, blocks, 8, 128), F32),
            pltpu.VMEM((2 * cz, points), BF16),
            pltpu.VMEM((points, cz), BF16),
            pltpu.VMEM((rows, points), F32),
            pltpu.VMEM((seg_rows, points), BF16),
            pltpu.VMEM((points, seg_rows), BF16),
            pltpu.VMEM((nproj, points), F32),
            pltpu.VMEM((seg_rows, 128), F32),
            pltpu.VMEM((seg_rows, 128), F32),
            pltpu.SemaphoreType.DMA((7,)),
            pltpu.SemaphoreType.DMA((groups,)),
            pltpu.SemaphoreType.DMA((DEGREE, groups, copies)),
            pltpu.SemaphoreType.DMA((DEGREE, groups, copies)),
        ],
        compiler_params=pltpu.CompilerParams(
            collective_id=0, has_side_effects=True, vmem_limit_bytes=63 * 1024 * 1024
        ),
    )(
        orbitals,
        potential,
        proj_values,
        point_cell.reshape(1, points),
        point_owner.reshape(1, points),
        point_slot.reshape(1, points),
        point_count,
        atom_energy,
    )


def solution(mesh):
    sizes = tuple(mesh.shape[name] for name in ("gx", "gy", "gz"))
    return jax.shard_map(
        functools.partial(body, sizes),
        mesh=mesh,
        in_specs=(
            P(None, "gx", "gy", "gz"),
            P("gx", "gy", "gz"),
            P(None, ("gx", "gy", "gz")),
            P(("gx", "gy", "gz")),
            P(("gx", "gy", "gz")),
            P(("gx", "gy", "gz")),
            P(("gx", "gy", "gz")),
            P(),
        ),
        out_specs=P(None, "gx", "gy", "gz"),
        check_vma=False,
    )
```
